128 devices in a mesh: section: 4 (over y), dp: 32 (over z, x, core).
Axes of the slice: x: 4, y: 4, z: 4, core: 2. Of those that a mesh axis runs over, the one named last changes fastest.
Arguments:
- old_master: float32 [49152, 4608], P(('section', 'dp')), may hold values from -0.44194174 to 0.44194174
- old_rows: int32 [49152], P(('section', 'dp')), may hold values from 0 to 49151, as said below
- gains: float32 [4, 2, 4608], P('section'), may hold values from 0.25 to 1.75
- hidden_in: bfloat16 [4, 2048, 4608], P('section', 'dp'), may hold values from -6 to 6
Outputs:
- new_master: float32 [49152, 4608], P(('section', 'dp'))
- hidden_out: bfloat16 [4, 2048, 4608], P('section', 'dp')
The draws below stay inside these ranges and needn't reach their ends.
Inputs may be any that keep to these rules, and one draw needn't show every extreme that they name: old_rows is a permutation of 0 to 49151; global row g belongs to device g // 384 (devices numbered section-major). Of the 384 entries of each device, exactly 257 belong to the device itself and exactly 1 to each other device.
All inputs are finite; a program needn't handle non-finite values.
Results may differ from the reference program's by a relative error of at most 0.018.
Values may be sent and summed in bfloat16 or wider, within the bound.
A program may use at most 128 MiB of HBM per device.

```python
import jax
import jax.numpy as jnp
from jax import lax

D = 4608
HD = 128
HOPS = 1
HEADS = 32
SLAB = 384
PEER = 1
KEEP = 257
MB_TOK = 2048
N_SECTION = 4
N_DP = 32
DEVICES = 128


def arrangement(key):
    perms = jax.vmap(lambda part_key: jax.random.permutation(part_key, SLAB))(jax.random.split(jax.random.fold_in(key, 11), DEVICES)).astype(jnp.int32)
    slots = jnp.arange(SLAB, dtype=jnp.int32)[None, :]
    owner_ids = jnp.arange(DEVICES, dtype=jnp.int32)[:, None]
    others = (slots - KEEP) // PEER
    other_holder = others + (others >= owner_ids).astype(jnp.int32)
    holder_seq = jnp.where(slots < KEEP, owner_ids, other_holder).astype(jnp.int32)
    assign = jnp.take_along_axis(holder_seq, jnp.argsort(perms, axis=1).astype(jnp.int32), axis=1)
    scores = assign.reshape(DEVICES * SLAB) * (DEVICES * SLAB) + jnp.arange(DEVICES * SLAB, dtype=jnp.int32)
    labels = jnp.argsort(scores).astype(jnp.int32).reshape(DEVICES, SLAB)
    shuffles = jax.vmap(lambda part_key: jax.random.permutation(part_key, SLAB))(jax.random.split(jax.random.fold_in(key, 12), DEVICES))
    return jnp.take_along_axis(labels, shuffles, axis=1).reshape(DEVICES * SLAB).astype(jnp.int32)


def draw_old_rows(key, part):
    return arrangement(key)


def draw_old_master(key, part):
    labels = arrangement(key)
    key = jax.random.fold_in(key, 3)
    within = labels % SLAB
    normals = jax.random.normal(key, (DEVICES * SLAB, D), jnp.float32)
    scales = jnp.where(within < 2 * HD, D ** (-0.5), (HD * N_DP) ** (-0.5))
    entries = jnp.clip(normals[labels], -6.0, 6.0)
    return entries * scales[:, None]


def block_scale(key, dims, cuts, smallest, largest):
    level, own = 1.0, jax.random.fold_in(key, 6)
    for position, parts in cuts:
        heights = jnp.exp(jax.random.uniform(jax.random.fold_in(own, position), (parts,), jnp.float32, smallest / len(cuts), largest / len(cuts)))
        level = level * jnp.repeat(heights, dims[position] // parts).reshape([-1 if axis == position else 1 for axis in range(len(dims))])
    return level


def centred(stream_key, dims, width, reach, pieces=(), kind=jnp.bfloat16):
    values = width * jax.random.normal(stream_key, dims, jnp.float32)
    if pieces:
        values = values * block_scale(stream_key, dims, pieces, -0.22, 0.18)
    return jnp.clip(values, -reach, reach).astype(kind)


def setup_inputs(seed: int = 0) -> dict:
    seeds = jax.random.split(jax.random.key(seed), 5)
    old_master = draw_old_master(jax.random.fold_in(seeds[4], 71), 0)
    old_rows = draw_old_rows(jax.random.fold_in(seeds[4], 71), 0)
    gains = jnp.clip(1.0 + 0.15 * jax.random.normal(seeds[2], (N_SECTION, 2, D), jnp.float32), 0.25, 1.75)
    hidden_in = centred(seeds[3], (N_SECTION, MB_TOK, D), 1.0, 6.0, ((0, 4), (1, 32)))
    return {"old_master": old_master, "old_rows": old_rows, "gains": gains, "hidden_in": hidden_in}


epsilon = 1e-06
score_scale = 1.0 / 12.0

def rounded(values):
    return lax.optimization_barrier(values.astype(jnp.bfloat16)).astype(jnp.float32)

def normed(values, gain):
    mean_square = lax.optimization_barrier(jnp.mean(values * values, axis=-1, keepdims=True))
    return values * lax.rsqrt(mean_square + epsilon) * gain

def apply_layer(block, gain_pair, hidden):
    weights = rounded(block)
    half_head = HD // 2
    query_w = weights[:, :HD]
    key_w = weights[:, HD:HD + half_head].reshape(HEADS // 2, HD, D)
    value_w = weights[:, HD + half_head:2 * HD].reshape(HEADS // 2, HD, D)
    output_w = weights[:, 2 * HD:]
    resident = hidden.astype(jnp.float32)
    scaled = rounded(normed(resident, gain_pair[0]))
    queries = rounded(jnp.einsum('td,hed->the', scaled, query_w))
    key_cols = jnp.repeat(rounded(jnp.einsum('td,ged->tge', scaled, key_w)), 2, axis=1)
    value_cols = jnp.repeat(rounded(jnp.einsum('td,ged->tge', scaled, value_w)), 2, axis=1)
    scores = jnp.einsum('the,she->hts', queries, key_cols) * score_scale
    length = hidden.shape[0]
    causal = jnp.arange(length)[:, None] >= jnp.arange(length)[None, :]
    scores = jnp.where(causal[None], scores, -1e+30)
    row_max = lax.optimization_barrier(jnp.max(scores, axis=-1, keepdims=True))
    exps = jnp.exp(scores - row_max)
    probabilities = rounded(exps / lax.optimization_barrier(jnp.sum(exps, axis=-1, keepdims=True)))
    attended = rounded(jnp.einsum('hts,she->the', probabilities, value_cols))
    terms = rounded(jnp.einsum('the,hed->htd', attended, output_w))
    summed = lax.optimization_barrier(jnp.sum(terms, axis=0))
    return (resident + normed(summed, gain_pair[1])).astype(jnp.bfloat16)

def reference(old_master, old_rows, gains, hidden_in):
    master = jnp.zeros_like(old_master).at[old_rows].set(old_master)
    blocks = master.reshape(N_SECTION, HEADS, SLAB, D)
    results = []
    for section_index in range(N_SECTION):
        micro_index = (section_index - HOPS) % N_SECTION
        current = hidden_in[micro_index]
        for hop_index in range(HOPS):
            layer_index = (micro_index + hop_index) % N_SECTION
            current = apply_layer(blocks[layer_index], gains[layer_index], current)
        results.append(current)
    return (master, jnp.stack(results))
```

```python
import jax
import jax.numpy as jnp
from jax import lax
from jax.experimental import pallas as pl
from jax.experimental.pallas import tpu as pltpu
from jax.sharding import PartitionSpec as P

MESH = pl.DeviceIdType.MESH
F32 = jnp.float32
BF16 = jnp.bfloat16

D = 4608
HD = 128
SLAB = 384
TOK = 2048
OWN_TOK = 64
HALF = D // 2
COLOR = HALF // 2
QUARTER = D // 4
DEVICES = 128
LABEL = SLAB
WIDE = D + LABEL
TILE = 384
QB = 256

epsilon = 1e-06
LOG2E = 1.4426950408889634
score_scale = LOG2E / 12.0

NT_DIMS = (((1,), (1,)), ((), ()))
TN_DIMS = (((0,), (0,)), ((), ()))


def iota(shape, dim):
    return lax.broadcasted_iota(jnp.int32, shape, dim)


def one_hot(mask):
    return jnp.where(mask, 1.0, 0.0).astype(BF16)


def mm(a, b, dims=None):
    if dims is None:
        return jnp.dot(a, b, preferred_element_type=F32)
    return lax.dot_general(a, b, dims, preferred_element_type=F32)


def span(index, size):
    return pl.ds(pl.multiple_of(index * size, size), size)


def layer_kernel(
    old_hbm, rows_ref, gains_ref, hid_ref, upd_ref, arr_hbm,
    stage, old_b, s0, b1, s1, b2, s2, b3, s3, b4, w, wp, nrm, xg, pown, psend, precv, z_qkv,
    att, hg, of, ow, sc, ps, rh, rf, mx, mixed, load_sem, loc_sem, send_sem, recv_sem,
):
    y = lax.axis_index("section")
    d = lax.axis_index("dp")
    c = lax.rem(d, 2)
    chip = lax.div(d, 2)
    x = lax.rem(chip, 4)
    z = lax.div(chip, 4)
    me = y * 32 + d

    def at(zz, xx, cc, yy=y):
        return (yy, (lax.rem(zz + 4, 4) * 4 + lax.rem(xx + 4, 4)) * 2 + cc)

    partner = at(z, x, 1 - c)
    ids = {}
    sent = []

    def slot(key):
        return ids.setdefault(key, len(ids))

    def send(key, src, dst, dev):
        n = slot(key)
        copy = pltpu.make_async_remote_copy(
            src_ref=src, dst_ref=dst, send_sem=send_sem.at[n], recv_sem=recv_sem.at[n],
            device_id=dev, device_id_type=MESH,
        )
        copy.start()
        sent.append(copy)

    def receive(key, dst):
        n = slot(key)
        pltpu.make_async_remote_copy(
            src_ref=dst, dst_ref=dst, send_sem=send_sem.at[n], recv_sem=recv_sem.at[n],
            device_id=partner, device_id_type=MESH,
        ).wait_recv()

    local_count = [0]

    def local(src, dst):
        copy = pltpu.make_async_copy(src, dst, loc_sem.at[local_count[0]])
        local_count[0] += 1
        copy.start()
        return copy

    def load(i):
        return pltpu.make_async_copy(
            old_hbm.at[pl.ds(i * 128, 128)], stage.at[i % 2], load_sem.at[i % 2]
        )

    load(0).start()
    load(1).start()

    barrier = pltpu.get_barrier_semaphore()
    greeted = [partner]
    for k in (1, 2, 3):
        greeted += [at(z, x, c, lax.rem(y + k, 4)), at(z + k, x, c), at(z, x + k, c)]
    for dev in greeted:
        pl.semaphore_signal(barrier, inc=1, device_id=dev, device_id_type=MESH)

    h = hid_ref[...].astype(F32)
    scale = lax.rsqrt(jnp.mean(h * h, axis=-1, keepdims=True) + epsilon)
    nrm[...] = (h * scale * gains_ref[0:1, :]).astype(BF16)
    pl.semaphore_wait(barrier, len(greeted))

    own_rows = pl.ds(pl.multiple_of(chip * 128 + c * 64, 64), 64)
    other_rows = pl.ds(pl.multiple_of(chip * 128 + (1 - c) * 64, 64), 64)
    send("norm", nrm.at[:, span(1 - c, HALF)], xg.at[own_rows], partner)
    own_copy = local(nrm.at[:, span(c, HALF)], xg.at[own_rows])

    def ag_place(colour, fk, sk, half):
        if colour == 0:
            cc = lax.rem(z + sk + 4, 4) * 4 + lax.rem(x + fk + 4, 4)
        else:
            cc = lax.rem(z + fk + 4, 4) * 4 + lax.rem(x + sk + 4, 4)
        if half is None:
            rows = pl.ds(pl.multiple_of(cc * 128, 128), 128)
        else:
            rows = pl.ds(pl.multiple_of(cc * 128 + half * 64, 64), 64)
        return xg.at[rows, pl.ds(colour * COLOR, COLOR)]

    def ag_send(colour, axis, step, fk, sk, half=None):
        along_x = (axis == "f") == (colour == 0)
        dev = at(z, x + step, c) if along_x else at(z + step, x, c)
        ref = ag_place(colour, fk, sk, half)
        send(("ag", colour, axis, step, fk % 4, sk % 4, half), ref, ref, dev)

    def ag_recv(colour, axis, step, fk, sk, half=None):
        key = ("ag", colour, axis, step, fk % 4, sk % 4, half)
        if axis == "f":
            fk = (fk - step) % 4
        else:
            sk = (sk - step) % 4
        receive(key, ag_place(colour, fk, sk, half))

    def part(step):
        return 0 if step == 1 else 1

    both = [(colour, step) for colour in (0, 1) for step in (1, -1)]

    own_copy.wait()
    receive("norm", xg.at[other_rows])
    for colour, step in both:
        ag_send(colour, "f", step, 0, 0)
    for colour, step in both:
        ag_send(colour, "s", step, 0, 0)

    rows = rows_ref[...]
    owner = jnp.floor((rows.astype(F32) + 0.5) * (1.0 / SLAB)).astype(jnp.int32)
    place = rows - owner * SLAB
    dest = iota((DEVICES, SLAB), 0)
    choose = one_hot((owner == dest) & (dest != me))
    place_t = one_hot(place == iota((SLAB, SLAB), 0))
    keep_t = one_hot((rows - me * SLAB) == iota((SLAB, SLAB), 0))
    for i in range(3):
        load(i).wait()

        def cast(j, carry):
            at_rows = pl.ds(pl.multiple_of(j * 16, 16), 16)
            old_b[pl.ds(pl.multiple_of(i * 128 + j * 16, 16), 16), :] = stage[i % 2, at_rows, :].astype(BF16)
            return carry

        lax.fori_loop(0, 8, cast, 0)
        if i == 0:
            load(2).start()

    def tiles(count, body):
        def one(j, carry):
            body(span(j, TILE))
            return carry

        lax.fori_loop(0, count, one, 0)

    def choose_rows(cols):
        s0[:, cols] = mm(choose, old_b[:, cols]).astype(BF16)

    tiles(D // TILE, choose_rows)
    s0[:, D:] = mm(choose, place_t, NT_DIMS).astype(BF16)

    def exchange_start(name, src, dst, index, dev):
        for k in (1, 2, 3):
            send((name, k), src.at[span(lax.rem(index + k, 4), 32)], dst.at[span(index, 32)], dev(k))
        return local(src.at[span(index, 32)], dst.at[span(index, 32)])

    def exchange_wait(name, dst, index, own):
        own.wait()
        for k in (1, 3, 2):
            receive((name, k), dst.at[span(lax.rem(index + 4 - k, 4), 32)])

    def regroup(src, dst, source_row):
        r = iota((DEVICES, DEVICES), 0)
        perm = one_hot(iota((DEVICES, DEVICES), 1) == source_row(r))

        def move(cols):
            dst[:, cols] = mm(perm, src[:, cols]).astype(BF16)

        tiles(WIDE // TILE, move)

    own_y = exchange_start("y", s0, b1, y, lambda k: at(z, x, c, lax.rem(y + k, 4)))

    for colour, step in both:
        ag_recv(colour, "f", step, 0, 0)
        ag_send(colour, "f", step, -step, 0, part(step))
        for step2 in (1, -1):
            ag_send(colour, "s", step2, -step, 0)
    for colour, step in both:
        ag_recv(colour, "s", step, 0, 0)
        ag_send(colour, "s", step, 0, -step, part(step))

    exchange_wait("y", b1, y, own_y)
    regroup(b1, s1, lambda r: ((r >> 3) & 3) * 32 + (r >> 5) * 8 + (r & 7))
    own_z = exchange_start("z", s1, b2, z, lambda k: at(z + k, x, c))

    for colour in (0, 1):
        for step in (1, -1):
            ag_recv(colour, "f", step, -step, 0, part(step))
        for step in (1, -1):
            ag_send(colour, "s", step, 2, 0)

    exchange_wait("z", b2, z, own_z)
    regroup(b2, s2, lambda r: ((r >> 3) & 3) * 32 + ((r >> 1) & 3) * 8 + (r >> 5) * 2 + (r & 1))
    own_x = exchange_start("x", s2, b3, x, lambda k: at(z, x + k, c))

    for fk in (-1, 1):
        for colour, step in both:
            ag_recv(colour, "s", step, fk, 0)
            ag_send(colour, "s", step, fk, -step, part(step))

    exchange_wait("x", b3, x, own_x)
    regroup(b3, s3, lambda r: (r & 63) * 2 + (r >> 6))
    send("core", s3.at[span(1 - c, 64)], b4.at[span(c, 64)], partner)
    own_c = local(s3.at[span(c, 64)], b4.at[span(c, 64)])

    for colour, step in both:
        ag_recv(colour, "s", step, 2, 0)
        ag_send(colour, "s", step, 2, -step, part(step))

    own_c.wait()
    receive("core", b4.at[span(1 - c, 64)])
    arr_copy = local(b4, arr_hbm)

    arrived = b4[:, D:]

    def place_rows(cols):
        w[:, cols] = (
            mm(keep_t, old_b[:, cols]) + mm(arrived, b4[:, cols], TN_DIMS)
        ).astype(BF16)

    tiles(D // TILE, place_rows)

    theirs = span(1 - c, HALF)
    ours = span(c, HALF)
    k_rows = pl.ds(pl.multiple_of(256 + 64 * c, 64), 64)
    v_rows = pl.ds(pl.multiple_of(384 + 64 * c, 64), 64)
    k_rows_p = pl.ds(pl.multiple_of(256 + 64 * (1 - c), 64), 64)
    v_rows_p = pl.ds(pl.multiple_of(384 + 64 * (1 - c), 64), 64)
    o_rows = span(c, 128)
    o_rows_p = span(1 - c, 128)
    send("wq", w.at[0:128, theirs], wp.at[128:256], partner)
    send("wk", w.at[128:192, theirs], wp.at[k_rows], partner)
    send("wv", w.at[192:256, theirs], wp.at[v_rows], partner)
    send("wo", w.at[256:384], of.at[o_rows], partner)
    own_w = [
        local(w.at[0:128, ours], wp.at[0:128]),
        local(w.at[128:192, ours], wp.at[k_rows]),
        local(w.at[192:256, ours], wp.at[v_rows]),
        local(w.at[256:384], of.at[o_rows]),
    ]

    for fk in (0, -1, 1, 2):
        for colour, step in both:
            ag_recv(colour, "s", step, fk, -step, part(step))

    for copy in own_w:
        copy.wait()
    receive("wq", wp.at[128:256])
    receive("wk", wp.at[k_rows_p])
    receive("wv", wp.at[v_rows_p])
    receive("wo", of.at[o_rows_p])

    fi = x + c * (z - x)
    si = z + c * (x - z)

    def along_f(k):
        return at(z + c * k, x + (1 - c) * k, c)

    def along_s(k):
        return at(z + (1 - c) * k, x + c * k, c)

    for k in (1, 3, 2):
        send(("ow", k), of.at[:, span(lax.rem(fi + k, 4), QUARTER)], ow.at[fi], along_f(k))
    own_o = local(of.at[:, span(fi, QUARTER)], ow.at[fi])

    group = 512

    def project(g):
        at_rows = pl.ds(g * group, group)
        acc = mm(xg[at_rows, :], wp[...], NT_DIMS)
        pown[at_rows, 0:128] = acc[:, 0:128]
        pown[at_rows, 128:384] = acc[:, 256:512]
        psend[at_rows, :] = acc[:, 128:512].astype(BF16)

    for g in range(TOK // group):
        project(g)
        at_rows = pl.ds(g * group, group)
        send(("proj", g), psend.at[at_rows], precv.at[at_rows], partner)

    def combine(g):
        at_rows = pl.ds(g * group, group)
        receive(("proj", g), precv.at[at_rows])
        z_qkv[at_rows, :] = (pown[at_rows, :] + precv[at_rows, :].astype(F32)).astype(BF16)

    def attend(qb):
        q = z_qkv[qb * QB : (qb + 1) * QB, 0:128]
        peak = None
        for kb in range(qb + 1):
            cols = slice(kb * QB, (kb + 1) * QB)
            s = mm(q, z_qkv[cols, 128:256], NT_DIMS) * score_scale
            if kb == qb:
                s = jnp.where(iota((QB, QB), 0) >= iota((QB, QB), 1), s, -1e30)
            sc[qb % 2, :, cols] = s
            top = jnp.maximum(s[:, 0:128], s[:, 128:256])
            peak = top if peak is None else jnp.maximum(peak, top)
        peak = jnp.max(peak, axis=-1, keepdims=True)
        total = None
        out = None
        for kb in range(qb + 1):
            cols = slice(kb * QB, (kb + 1) * QB)
            e = jnp.exp2(sc[qb % 2, :, cols] - peak)
            add = e[:, 0:128] + e[:, 128:256]
            total = add if total is None else total + add
            o = mm(e.astype(BF16), z_qkv[cols, 256:384])
            out = o if out is None else out + o
        total = jnp.sum(total, axis=-1, keepdims=True)
        out = (out / total).astype(BF16)
        for i in range(QB // 128):
            ci = qb * (QB // 128) + i
            turned = (ci % 4) * 4 + ci // 4
            att[0, ci * 64 : ci * 64 + 64, :] = out[i * 128 : i * 128 + 64]
            att[1, turned * 64 : turned * 64 + 64, :] = out[i * 128 + 64 : i * 128 + 128]

    for g in range(TOK // group):
        combine(g)
    for qb in range(TOK // QB):
        attend(qb)

    head_cols = span(c, 128)
    head_cols_p = span(1 - c, 128)
    send("att", att.at[1 - c], hg.at[si, :, head_cols], partner)
    own_a = local(att.at[c], hg.at[fi, :, head_cols])
    own_a.wait()
    receive("att", hg.at[fi, :, head_cols_p])

    def f_at(k):
        return lax.rem(fi + k + 4, 4)

    for step in (1, -1):
        send(("hg", step), hg.at[fi], hg.at[fi], along_f(step))
    for step in (1, -1):
        receive(("hg", step), hg.at[f_at(-step)])
        rows_f = pl.ds(part(step) * 512, 512)
        ref = hg.at[f_at(-step), rows_f]
        send(("hg2", step), ref, ref, along_f(step))
    for step in (1, -1):
        receive(("hg2", step), hg.at[f_at(2), pl.ds(part(step) * 512, 512)])

    own_o.wait()
    for k in (1, 3, 2):
        receive(("ow", k), ow.at[lax.rem(fi + 4 - k, 4)])

    def partial(j, cols):
        sg = lax.rem(si + j + 4, 4)
        at_rows = span(sg, 256)
        acc = None
        for f in range(4):
            o = mm(hg[f, at_rows, :], ow[f, :, cols])
            acc = o if acc is None else acc + o
        return acc

    def far(cols):
        ps[0, :, cols] = partial(2, cols).astype(BF16)

    tiles(QUARTER // TILE, far)
    send(("rh", 1), ps.at[0, 0:128], rh.at[0], along_s(1))
    send(("rh", -1), ps.at[0, 128:256], rh.at[1], along_s(-1))

    receive(("rh", 1), rh.at[0])

    def plus(cols):
        acc = partial(1, cols)
        ps[1, 0:128, cols] = (acc[0:128] + rh[0, :, cols].astype(F32)).astype(BF16)
        ps[1, 128:256, cols] = acc[128:256].astype(BF16)

    tiles(QUARTER // TILE, plus)
    send(("rf", 1), ps.at[1], rf.at[0], along_s(1))

    receive(("rh", -1), rh.at[1])

    def minus(cols):
        acc = partial(-1, cols)
        ps[2, 0:128, cols] = acc[0:128].astype(BF16)
        ps[2, 128:256, cols] = (acc[128:256] + rh[1, :, cols].astype(F32)).astype(BF16)

    tiles(QUARTER // TILE, minus)
    send(("rf", -1), ps.at[2], rf.at[1], along_s(-1))

    receive(("rf", 1), rf.at[0])
    receive(("rf", -1), rf.at[1])

    def near(cols):
        acc = partial(0, cols)
        mx[:, cols] = (acc + rf[0, :, cols].astype(F32) + rf[1, :, cols].astype(F32)).astype(BF16)

    tiles(QUARTER // TILE, near)

    for k in (1, 3, 2):
        send(("mx", k), mx.at[span(lax.rem(fi + k, 4), 64)], mixed.at[:, span(fi, QUARTER)], along_f(k))
    own_m = local(mx.at[span(fi, 64)], mixed.at[:, span(fi, QUARTER)])
    own_m.wait()
    for k in (1, 3, 2):
        receive(("mx", k), mixed.at[:, span(lax.rem(fi + 4 - k, 4), QUARTER)])

    m = mixed[...].astype(F32)
    scale2 = lax.rsqrt(jnp.mean(m * m, axis=-1, keepdims=True) + epsilon)
    upd_ref[...] = (hid_ref[...].astype(F32) + m * scale2 * gains_ref[1:2, :]).astype(BF16)

    arr_copy.wait()
    for copy in sent:
        copy.wait_send()


def layer(old_master, rows, gains, hidden):
    vmem = pl.BlockSpec(memory_space=pltpu.VMEM)
    anywhere = pl.BlockSpec(memory_space=pl.ANY)
    exch = pltpu.VMEM((DEVICES, WIDE), BF16)
    return pl.pallas_call(
        layer_kernel,
        out_shape=(
            jax.ShapeDtypeStruct((OWN_TOK, D), BF16),
            jax.ShapeDtypeStruct((DEVICES, WIDE), BF16),
        ),
        in_specs=[anywhere, vmem, vmem, vmem],
        out_specs=(vmem, anywhere),
        scratch_shapes=[
            pltpu.VMEM((2, 128, D), F32),
            pltpu.VMEM((SLAB, D), BF16),
            exch, exch, exch, exch, exch, exch, exch, exch,
            pltpu.VMEM((SLAB, D), BF16),
            pltpu.VMEM((512, HALF), BF16),
            pltpu.VMEM((OWN_TOK, D), BF16),
            pltpu.VMEM((TOK, HALF), BF16),
            pltpu.VMEM((TOK, 384), F32),
            pltpu.VMEM((TOK, 384), BF16),
            pltpu.VMEM((TOK, 384), BF16),
            pltpu.VMEM((TOK, 384), BF16),
            pltpu.VMEM((2, TOK // 2, 128), BF16),
            pltpu.VMEM((4, TOK // 2, 256), BF16),
            pltpu.VMEM((256, D), BF16),
            pltpu.VMEM((4, 256, QUARTER), BF16),
            pltpu.VMEM((2, QB, TOK), F32),
            pltpu.VMEM((3, 256, QUARTER), BF16),
            pltpu.VMEM((2, 128, QUARTER), BF16),
            pltpu.VMEM((2, 256, QUARTER), BF16),
            pltpu.VMEM((256, QUARTER), BF16),
            pltpu.VMEM((OWN_TOK, D), BF16),
            pltpu.SemaphoreType.DMA((2,)),
            pltpu.SemaphoreType.DMA((16,)),
            pltpu.SemaphoreType.DMA((96,)),
            pltpu.SemaphoreType.DMA((96,)),
        ],
        compiler_params=pltpu.CompilerParams(
            collective_id=0, has_side_effects=True, vmem_limit_bytes=62 * 1024 * 1024
        ),
    )(old_master, rows, gains, hidden)


def place_kernel(old_ref, rows_ref, arr_ref, lab_ref, out_ref):
    me = lax.axis_index("section") * 32 + lax.axis_index("dp")
    keep_t = one_hot((rows_ref[...] - me * SLAB) == iota((SLAB, SLAB), 0))
    v = old_ref[...]
    hi = v.astype(BF16)
    rest = v - hi.astype(F32)
    mid = rest.astype(BF16)
    low = (rest - mid.astype(F32)).astype(BF16)
    kept = (mm(keep_t, hi) + mm(keep_t, mid)) + mm(keep_t, low)
    out_ref[...] = kept + mm(lab_ref[...], arr_ref[...], TN_DIMS)


def place_master(old_master, rows, arrived):
    width = 512
    return pl.pallas_call(
        place_kernel,
        grid=(D // width,),
        out_shape=jax.ShapeDtypeStruct((SLAB, D), F32),
        in_specs=[
            pl.BlockSpec((SLAB, width), lambda j: (0, j)),
            pl.BlockSpec((1, SLAB), lambda j: (0, 0)),
            pl.BlockSpec((DEVICES, width), lambda j: (0, j)),
            pl.BlockSpec((DEVICES, LABEL), lambda j: (0, D // LABEL)),
        ],
        out_specs=pl.BlockSpec((SLAB, width), lambda j: (0, j)),
        compiler_params=pltpu.CompilerParams(vmem_limit_bytes=32 * 1024 * 1024),
        cost_estimate=pl.CostEstimate(flops=5_000_000_000, bytes_accessed=15_000_000, transcendentals=0),
    )(old_master, rows, arrived, arrived)


def body(old_master, old_rows, gains, hidden_in):
    rows = old_rows.reshape(1, SLAB)
    updated, arrived = layer(old_master, rows, gains[0], hidden_in[0])
    size = lax.axis_size("section")
    passed = lax.ppermute(updated, "section", [(i, (i + 1) % size) for i in range(size)])
    master = place_master(old_master, rows, arrived)
    return (master, passed[None])


def solution(mesh):
    in_specs = (
        P(("section", "dp"), None),
        P(("section", "dp")),
        P("section", None, None),
        P("section", "dp", None),
    )
    out_specs = (P(("section", "dp"), None), P("section", "dp", None))
    return jax.shard_map(body, mesh=mesh, in_specs=in_specs, out_specs=out_specs, check_vma=False)
```

```python
import jax
import jax.numpy as jnp
from jax import lax
from jax.experimental import pallas as pl
from jax.experimental.pallas import tpu as pltpu
from jax.sharding import PartitionSpec as P

MESH = pl.DeviceIdType.MESH
F32 = jnp.float32
BF16 = jnp.bfloat16

D = 4608
HD = 128
SLAB = 384
TOK = 2048
OWN_TOK = 64
HALF = D // 2
COLOR = HALF // 2
QUARTER = D // 4
DEVICES = 128
PIECE = HALF + 128
TILE = 384
GROUP = 512
QB = 256

epsilon = 1e-06
LOG2E = 1.4426950408889634
score_scale = LOG2E / 12.0

NT_DIMS = (((1,), (1,)), ((), ()))
TN_DIMS = (((0,), (0,)), ((), ()))


def iota(shape, dim):
    return lax.broadcasted_iota(jnp.int32, shape, dim)


def one_hot(mask):
    return jnp.where(mask, 1.0, 0.0).astype(BF16)


def mm(a, b, dims=None):
    if dims is None:
        return jnp.dot(a, b, preferred_element_type=F32)
    return lax.dot_general(a, b, dims, preferred_element_type=F32)


def span(index, size):
    return pl.ds(pl.multiple_of(index * size, size), size)


def merge(left, right):
    n = left.shape[1]
    pair = jnp.concatenate([left.reshape(16, 8, n), right.reshape(16, 8, n)], axis=1)
    return pair.reshape(256, n).astype(BF16)


def layer_kernel(
    old_hbm, rows_ref, gains_ref, hid_ref, master_hbm, out_ref,
    old_f, old_b, s1, b1, s2, b3, w, wp, nrm, xg, acc, psend, precv, z_qkv,
    att, hg, of, ow, sc, part_f, ps, rh, rf, mx, mixed, hid_y, gains_y,
    load_sem, loc_sem, send_sem, recv_sem,
):
    y = lax.axis_index("section")
    d = lax.axis_index("dp")
    c = lax.rem(d, 2)
    chip = lax.div(d, 2)
    x = lax.rem(chip, 4)
    z = lax.div(chip, 4)
    me = y * 32 + d

    def at(zz, xx, cc, yy=y):
        return (lax.rem(yy + 4, 4), (lax.rem(zz + 4, 4) * 4 + lax.rem(xx + 4, 4)) * 2 + cc)

    partner = at(z, x, 1 - c)
    ids = {}
    sent = []

    def slot(key):
        return ids.setdefault(key, len(ids))

    def send(key, src, dst, dev):
        n = slot(key)
        copy = pltpu.make_async_remote_copy(
            src_ref=src, dst_ref=dst, send_sem=send_sem.at[n], recv_sem=recv_sem.at[n],
            device_id=dev, device_id_type=MESH,
        )
        copy.start()
        sent.append(copy)

    def receive(key, dst):
        n = slot(key)
        pltpu.make_async_remote_copy(
            src_ref=dst, dst_ref=dst, send_sem=send_sem.at[n], recv_sem=recv_sem.at[n],
            device_id=partner, device_id_type=MESH,
        ).wait_recv()

    local_count = [0]

    def local(src, dst):
        copy = pltpu.make_async_copy(src, dst, loc_sem.at[local_count[0]])
        local_count[0] += 1
        copy.start()
        return copy

    def load(i):
        at_rows = pl.ds(i * 128, 128)
        return pltpu.make_async_copy(old_hbm.at[at_rows], old_f.at[at_rows], load_sem.at[i])

    for i in range(3):
        load(i).start()

    barrier = pltpu.get_barrier_semaphore()
    greeted = [at(z + j, x, c, y + i) for i in range(4) for j in range(4) if i or j]
    greeted += [at(z, x, 1 - c)]
    for k in (1, 2, 3):
        greeted += [at(z, x + k, c), at(z, x + k, 1 - c), at(z, x + k, c, y + 1), at(z, x + k, c, y + 3)]
    for dev in greeted:
        pl.semaphore_signal(barrier, inc=1, device_id=dev, device_id_type=MESH)

    h = hid_ref[...].astype(F32)
    scale = lax.rsqrt(jnp.mean(h * h, axis=-1, keepdims=True) + epsilon)
    nrm[...] = (h * scale * gains_ref[0:1, :]).astype(BF16)
    pl.semaphore_wait(barrier, len(greeted))

    own_rows = pl.ds(pl.multiple_of(chip * 128 + c * 64, 64), 64)
    other_rows = pl.ds(pl.multiple_of(chip * 128 + (1 - c) * 64, 64), 64)
    send("norm", nrm.at[:, span(1 - c, HALF)], xg.at[own_rows], partner)
    own_copy = local(nrm.at[:, span(c, HALF)], xg.at[own_rows])

    def ag_place(colour, fk, sk, half):
        if colour == 0:
            cc = lax.rem(z + sk + 4, 4) * 4 + lax.rem(x + fk + 4, 4)
        else:
            cc = lax.rem(z + fk + 4, 4) * 4 + lax.rem(x + sk + 4, 4)
        if half is None:
            rows = pl.ds(pl.multiple_of(cc * 128, 128), 128)
        else:
            rows = pl.ds(pl.multiple_of(cc * 128 + half * 64, 64), 64)
        return xg.at[rows, pl.ds(colour * COLOR, COLOR)]

    def ag_send(colour, axis, step, fk, sk, half=None):
        along_x = (axis == "f") == (colour == 0)
        dev = at(z, x + step, c) if along_x else at(z + step, x, c)
        ref = ag_place(colour, fk, sk, half)
        send(("ag", colour, axis, step, fk % 4, sk % 4, half), ref, ref, dev)

    def ag_recv(colour, axis, step, fk, sk, half=None):
        key = ("ag", colour, axis, step, fk % 4, sk % 4, half)
        if axis == "f":
            fk = (fk - step) % 4
        else:
            sk = (sk - step) % 4
        receive(key, ag_place(colour, fk, sk, half))

    def part(step):
        return 0 if step == 1 else 1

    both = [(colour, step) for colour in (0, 1) for step in (1, -1)]

    def tiles(count, body, size=TILE):
        def one(j, carry):
            body(span(j, size))
            return carry

        lax.fori_loop(0, count, one, 0)

    own_copy.wait()
    receive("norm", xg.at[other_rows])
    for colour, step in both:
        ag_send(colour, "f", step, 0, 0)
    for colour, step in both:
        ag_send(colour, "s", step, 0, 0)

    rows = rows_ref[...]
    owner = jnp.floor((rows.astype(F32) + 0.5) * (1.0 / SLAB)).astype(jnp.int32)
    place = rows - owner * SLAB
    dest = iota((DEVICES, SLAB), 0)
    choose = one_hot((owner == dest) & (dest != me))
    keep_t = one_hot((rows - me * SLAB) == iota((SLAB, SLAB), 0))
    low_t = one_hot((place & 127) == iota((128, SLAB), 0))
    high_t = one_hot((place >> 7) == iota((128, SLAB), 0))
    for i in range(3):
        load(i).wait()

        def cast(j, carry):
            at_rows = pl.ds(pl.multiple_of(i * 128 + j * 16, 16), 16)
            old_b[at_rows, :] = old_f[at_rows, :].astype(BF16)
            return carry

        lax.fori_loop(0, 8, cast, 0)

    def choose_rows(j, carry):
        cols = span(j, TILE)
        cols2 = pl.ds(pl.multiple_of(HALF + j * TILE, TILE), TILE)
        s1[:, cols] = merge(mm(choose, old_b[:, cols]), mm(choose, old_b[:, cols2]))
        return carry

    lax.fori_loop(0, HALF // TILE, choose_rows, 0)
    s1[:, HALF:] = merge(mm(choose, low_t, NT_DIMS), mm(choose, high_t, NT_DIMS))

    group_me = y * 4 + z
    across = [(i, j) for i in (2, 1, 3, 0) for j in (2, 1, 3, 0) if i or j]
    for i, j in across:
        g = lax.rem(y + i, 4) * 4 + lax.rem(z + j, 4)
        send(("yz", i, j), s1.at[span(g, 16)], b1.at[span(group_me, 16)], at(z + j, x, c, y + i))
    own_yz = local(s1.at[span(group_me, 16)], b1.at[span(group_me, 16)])

    send("hid", hid_ref, hid_y, at(z, x, c, y + 1))
    send("gains", gains_ref, gains_y, at(z, x, c, y + 1))

    def keep_rows(cols):
        high = old_b[:, cols]
        rest = old_f[:, cols] - high.astype(F32)
        mid = rest.astype(BF16)
        low = (rest - mid.astype(F32)).astype(BF16)
        old_f[:, cols] = (mm(keep_t, high) + mm(keep_t, mid)) + mm(keep_t, low)

    lax.fori_loop(0, 6, lambda j, t: (keep_rows(span(j, TILE)), t)[1], 0)

    for colour, step in both:
        ag_recv(colour, "f", step, 0, 0)
        ag_send(colour, "f", step, -step, 0, part(step))
        for step2 in (1, -1):
            ag_send(colour, "s", step2, -step, 0)
    for colour, step in both:
        ag_recv(colour, "s", step, 0, 0)
        ag_send(colour, "s", step, 0, -step, part(step))

    lax.fori_loop(6, D // TILE, lambda j, t: (keep_rows(span(j, TILE)), t)[1], 0)

    own_yz.wait()
    for i, j in across:
        g = lax.rem(y + 4 - i, 4) * 4 + lax.rem(z + 4 - j, 4)
        receive(("yz", i, j), b1.at[span(g, 16)])

    r2 = iota((DEVICES, 256), 0)
    from_row = (r2 & 15) * 16 + (r2 >> 4)
    perm_l = one_hot(iota((DEVICES, 256), 1) == from_row)
    perm_r = one_hot(iota((DEVICES, 256), 1) == from_row + 8)

    def regroup(j, carry):
        cols = span(j, TILE)
        cols2 = pl.ds(pl.multiple_of(HALF + j * TILE, TILE), TILE)
        piece = b1[:, cols]
        s2[:, cols] = mm(perm_l, piece).astype(BF16)
        s2[:, cols2] = mm(perm_r, piece).astype(BF16)
        return carry

    lax.fori_loop(0, HALF // TILE, regroup, 0)
    s2[:, D : D + 128] = mm(perm_l, b1[:, HALF:]).astype(BF16)
    s2[:, D + 128 :] = mm(perm_r, b1[:, HALF:]).astype(BF16)

    e_me = x * 2 + c
    for m in (4, 3, 5, 2, 6, 1, 7):
        e = lax.rem(e_me + m, 8)
        send(("xc", m), s2.at[span(e, 16)], b3.at[span(e_me, 16)], at(z, lax.div(e, 2), lax.rem(e, 2)))
    own_xc = local(s2.at[span(e_me, 16)], b3.at[span(e_me, 16)])

    for colour in (0, 1):
        for step in (1, -1):
            ag_recv(colour, "f", step, -step, 0, part(step))
        for step in (1, -1):
            ag_send(colour, "s", step, 2, 0)
    for fk in (-1, 1):
        for colour, step in both:
            ag_recv(colour, "s", step, fk, 0)
            ag_send(colour, "s", step, fk, -step, part(step))

    own_xc.wait()
    for m in (4, 3, 5, 2, 6, 1, 7):
        receive(("xc", m), b3.at[span(lax.rem(e_me + 8 - m, 8), 16)])

    low_lab = b3[:, D : D + 128]
    high_lab = b3[:, D + 128 :]
    arrived = jnp.concatenate([low_lab * high_lab[:, a : a + 1] for a in range(3)], axis=1)

    def place_rows(cols):
        m = old_f[:, cols] + mm(arrived, b3[:, cols], TN_DIMS)
        old_f[:, cols] = m
        w[:, cols] = m.astype(BF16)

    tiles(D // TILE, place_rows)
    master_copy = local(old_f, master_hbm)

    theirs = span(1 - c, HALF)
    ours = span(c, HALF)
    k_rows = pl.ds(pl.multiple_of(256 + 64 * c, 64), 64)
    v_rows = pl.ds(pl.multiple_of(384 + 64 * c, 64), 64)
    k_rows_p = pl.ds(pl.multiple_of(256 + 64 * (1 - c), 64), 64)
    v_rows_p = pl.ds(pl.multiple_of(384 + 64 * (1 - c), 64), 64)
    o_rows = span(c, 128)
    o_rows_p = span(1 - c, 128)
    send("wq", w.at[0:128, theirs], wp.at[128:256], partner)
    send("wk", w.at[128:192, theirs], wp.at[k_rows], partner)
    send("wv", w.at[192:256, theirs], wp.at[v_rows], partner)
    send("wo", w.at[256:384], of.at[o_rows], partner)
    own_w = [
        local(w.at[0:128, ours], wp.at[0:128]),
        local(w.at[128:192, ours], wp.at[k_rows]),
        local(w.at[192:256, ours], wp.at[v_rows]),
        local(w.at[256:384], of.at[o_rows]),
    ]

    for colour, step in both:
        ag_recv(colour, "s", step, 2, 0)
        ag_send(colour, "s", step, 2, -step, part(step))

    for copy in own_w:
        copy.wait()
    receive("wq", wp.at[128:256])
    receive("wk", wp.at[k_rows_p])
    receive("wv", wp.at[v_rows_p])
    receive("wo", of.at[o_rows_p])

    fi = x + c * (z - x)
    si = z + c * (x - z)

    def along_f(k, yy=y):
        return at(z + c * k, x + (1 - c) * k, c, yy)

    def along_s(k):
        return at(z + (1 - c) * k, x + c * k, c)

    for k in (2, 1, 3):
        send(("ow", k), of.at[:, span(lax.rem(fi + k, 4), QUARTER)], ow.at[fi], along_f(k))
    own_o = local(of.at[:, span(fi, QUARTER)], ow.at[fi])

    def project(colour, fk, fresh):
        if colour == 0:
            xx = lax.rem(x + fk + 4, 4)
            places = [pl.ds(pl.multiple_of((q * 4 + xx) * 128, 128), 128) for q in range(4)]
        else:
            zz = lax.rem(z + fk + 4, 4)
            places = [pl.ds(pl.multiple_of((zz * 4 + q) * 128, 128), 128) for q in range(4)]
        cols = slice(colour * COLOR, (colour + 1) * COLOR)
        block = jnp.concatenate([xg[p, cols] for p in places], axis=0)
        out = mm(block, wp[:, cols], NT_DIMS)
        for q, p in enumerate(places):
            piece = out[q * 128 : (q + 1) * 128]
            acc[p, :] = piece if fresh else acc[p, :] + piece

    for colour in (0, 1):
        for fk in (0, -1, 1, 2):
            for step in (1, -1):
                ag_recv(colour, "s", step, fk, -step, part(step))
            project(colour, fk, colour == 0)

    for g in range(4):
        at_rows = pl.ds(g * GROUP, GROUP)
        psend[at_rows, :] = acc[at_rows, 128:512].astype(BF16)
        send(("proj", g), psend.at[at_rows], precv.at[at_rows], partner)

    def combine(g):
        at_rows = pl.ds(g * GROUP, GROUP)
        receive(("proj", g), precv.at[at_rows])
        q = acc[at_rows, 0:128] + precv[at_rows, 0:128].astype(F32)
        kv = acc[at_rows, 256:512] + precv[at_rows, 128:384].astype(F32)
        z_qkv[at_rows, 0:128] = q.astype(BF16)
        z_qkv[at_rows, 128:384] = kv.astype(BF16)

    def attend(qb):
        q = z_qkv[qb * QB : (qb + 1) * QB, 0:128]
        peak = None
        for kb in range(qb + 1):
            cols = slice(kb * QB, (kb + 1) * QB)
            s = mm(q, z_qkv[cols, 128:256], NT_DIMS) * score_scale
            if kb == qb:
                s = jnp.where(iota((QB, QB), 0) >= iota((QB, QB), 1), s, -1e30)
            sc[:, cols] = s
            top = jnp.maximum(s[:, 0:128], s[:, 128:256])
            peak = top if peak is None else jnp.maximum(peak, top)
        peak = jnp.max(peak, axis=-1, keepdims=True)
        total = None
        out = None
        for kb in range(qb + 1):
            cols = slice(kb * QB, (kb + 1) * QB)
            e = jnp.exp2(sc[:, cols] - peak)
            add = e[:, 0:128] + e[:, 128:256]
            total = add if total is None else total + add
            o = mm(e.astype(BF16), z_qkv[cols, 256:384])
            out = o if out is None else out + o
        total = jnp.sum(total, axis=-1, keepdims=True)
        out = (out / total).astype(BF16)
        for i in range(QB // 128):
            ci = qb * (QB // 128) + i
            att[0, ci * 64 : ci * 64 + 64, :] = out[i * 128 : i * 128 + 64]
            att[1, ci * 64 : ci * 64 + 64, :] = out[i * 128 + 64 : i * 128 + 128]

    head_cols = span(c, 128)
    head_cols_p = span(1 - c, 128)
    own_a = {}

    def f_at(k):
        return lax.rem(fi + k + 4, 4)

    def rows_g(g, half=None):
        return pl.ds(g * 256, 256) if half is None else pl.ds(g * 256 + half * 128, 128)

    def gather_1(g):
        send(("att", g), att.at[1 - c, rows_g(g)], hg.at[si, rows_g(g), head_cols], partner)
        own_a[g] = local(att.at[c, rows_g(g)], hg.at[fi, rows_g(g), head_cols])

    def gather_2(g):
        own_a[g].wait()
        receive(("att", g), hg.at[fi, rows_g(g), head_cols_p])
        for step in (1, -1):
            ref = hg.at[fi, rows_g(g)]
            send(("hg", step, g), ref, ref, along_f(step))

    def gather_3(g):
        for step in (1, -1):
            receive(("hg", step, g), hg.at[f_at(-step), rows_g(g)])
            ref = hg.at[f_at(-step), rows_g(g, part(step))]
            send(("hg2", step, g), ref, ref, along_f(step))

    combine(0)
    attend(0)
    attend(1)
    gather_1(0)
    combine(1)
    attend(2)
    gather_2(0)
    attend(3)
    gather_1(1)
    gather_3(0)
    combine(2)
    attend(4)
    gather_2(1)
    attend(5)
    gather_1(2)
    gather_3(1)
    combine(3)
    attend(6)
    gather_2(2)
    attend(7)
    gather_1(3)
    gather_3(2)
    gather_2(3)
    gather_3(3)
    for g in range(4):
        for step in (1, -1):
            receive(("hg2", step, g), hg.at[f_at(2), rows_g(g, part(step))])

    own_o.wait()
    for k in (1, 3, 2):
        receive(("ow", k), ow.at[lax.rem(fi + 4 - k, 4)])

    def partial(j, cols):
        sg = lax.rem(si + j + 4, 4)
        out = None
        for f in range(4):
            block = jnp.concatenate(
                [
                    hg[f, pl.ds(pl.multiple_of(sg * (256 - 192 * c) + q * (64 + 192 * c), 64), 64), :]
                    for q in range(4)
                ],
                axis=0,
            )
            o = mm(block, ow[f, :, cols])
            out = o if out is None else out + o
        return out

    order = (2, 1, 3, 0)

    def piece(k, half=None):
        q = f_at(k)
        if half is None:
            return pl.ds(pl.multiple_of(q * 64, 64), 64)
        return pl.ds(pl.multiple_of(q * 64 + half * 32, 32), 32)

    def far(cols):
        ps[0, :, cols] = partial(2, cols).astype(BF16)

    tiles(QUARTER // TILE, far)
    for k in order:
        for step in (1, -1):
            rows_k = piece(k, part(step))
            send(("rh", step, k), ps.at[0, rows_k], rh.at[part(step), rows_k], along_s(step))

    for n, j in ((1, 1), (2, -1), (0, 0)):

        def other(cols):
            part_f[n, :, cols] = partial(j, cols)

        tiles(QUARTER // TILE, other)

    for k in order:
        for step in (1, -1):
            mine = piece(k, part(step))
            rest = piece(k, 1 - part(step))
            n = 1 + part(step)
            receive(("rh", step, k), rh.at[part(step), mine])
            ps[n, mine, :] = (part_f[n, mine, :] + rh[part(step), mine, :].astype(F32)).astype(BF16)
            ps[n, rest, :] = part_f[n, rest, :].astype(BF16)
            send(("rf", step, k), ps.at[n, piece(k)], rf.at[part(step), piece(k)], along_s(step))

    for k in order:
        rows_k = piece(k)
        for step in (1, -1):
            receive(("rf", step, k), rf.at[part(step), rows_k])
        total = part_f[0, rows_k, :] + rf[0, rows_k, :].astype(F32) + rf[1, rows_k, :].astype(F32)
        mx[rows_k, :] = total.astype(BF16)
        send(("mx", k), mx.at[rows_k], mixed.at[:, span(fi, QUARTER)], along_f(k, y + 1))

    receive("hid", hid_y)
    receive("gains", gains_y)
    for k in order:
        receive(("mx", k), mixed.at[:, span(lax.rem(fi + 4 - k, 4), QUARTER)])

    m = mixed[...].astype(F32)
    scale2 = lax.rsqrt(jnp.mean(m * m, axis=-1, keepdims=True) + epsilon)
    out_ref[...] = (hid_y[...].astype(F32) + m * scale2 * gains_y[1:2, :]).astype(BF16)

    master_copy.wait()
    for copy in sent:
        copy.wait_send()


def layer(old_master, rows, gains, hidden):
    vmem = pl.BlockSpec(memory_space=pltpu.VMEM)
    anywhere = pl.BlockSpec(memory_space=pl.ANY)
    return pl.pallas_call(
        layer_kernel,
        out_shape=(
            jax.ShapeDtypeStruct((SLAB, D), F32),
            jax.ShapeDtypeStruct((OWN_TOK, D), BF16),
        ),
        in_specs=[anywhere, vmem, vmem, vmem],
        out_specs=(anywhere, vmem),
        scratch_shapes=[
            pltpu.VMEM((SLAB, D), F32),
            pltpu.VMEM((SLAB, D), BF16),
            pltpu.VMEM((256, PIECE), BF16),
            pltpu.VMEM((256, PIECE), BF16),
            pltpu.VMEM((DEVICES, 2 * PIECE), BF16),
            pltpu.VMEM((DEVICES, 2 * PIECE), BF16),
            pltpu.VMEM((SLAB, D), BF16),
            pltpu.VMEM((512, HALF), BF16),
            pltpu.VMEM((OWN_TOK, D), BF16),
            pltpu.VMEM((TOK, HALF), BF16),
            pltpu.VMEM((TOK, 512), F32),
            pltpu.VMEM((TOK, 384), BF16),
            pltpu.VMEM((TOK, 384), BF16),
            pltpu.VMEM((TOK, 384), BF16),
            pltpu.VMEM((2, TOK // 2, 128), BF16),
            pltpu.VMEM((4, TOK // 2, 256), BF16),
            pltpu.VMEM((256, D), BF16),
            pltpu.VMEM((4, 256, QUARTER), BF16),
            pltpu.VMEM((QB, TOK), F32),
            pltpu.VMEM((3, 256, QUARTER), F32),
            pltpu.VMEM((3, 256, QUARTER), BF16),
            pltpu.VMEM((2, 256, QUARTER), BF16),
            pltpu.VMEM((2, 256, QUARTER), BF16),
            pltpu.VMEM((256, QUARTER), BF16),
            pltpu.VMEM((OWN_TOK, D), BF16),
            pltpu.VMEM((OWN_TOK, D), BF16),
            pltpu.VMEM((2, D), F32),
            pltpu.SemaphoreType.DMA((3,)),
            pltpu.SemaphoreType.DMA((16,)),
            pltpu.SemaphoreType.DMA((128,)),
            pltpu.SemaphoreType.DMA((128,)),
        ],
        compiler_params=pltpu.CompilerParams(
            collective_id=0, has_side_effects=True, vmem_limit_bytes=63 * 1024 * 1024
        ),
    )(old_master, rows, gains, hidden)


def body(old_master, old_rows, gains, hidden_in):
    rows = old_rows.reshape(1, SLAB)
    master, hidden_out = layer(old_master, rows, gains[0], hidden_in[0])
    return (master, hidden_out[None])


def solution(mesh):
    in_specs = (
        P(("section", "dp"), None),
        P(("section", "dp")),
        P("section", None, None),
        P("section", "dp", None),
    )
    out_specs = (P(("section", "dp"), None), P("section", "dp", None))
    return jax.shard_map(body, mesh=mesh, in_specs=in_specs, out_specs=out_specs, check_vma=False)
```

```python
import jax
import jax.numpy as jnp
from jax import lax
from jax.experimental import pallas as pl
from jax.experimental.pallas import tpu as pltpu
from jax.sharding import PartitionSpec as P

MESH = pl.DeviceIdType.MESH
F32 = jnp.float32
BF16 = jnp.bfloat16

D = 4608
HD = 128
SLAB = 384
TOK = 2048
OWN_TOK = 64
HALF = D // 2
COLOR = HALF // 2
QUARTER = D // 4
DEVICES = 128
PIECE = HALF + 128
TILE = 384
GROUP = 512
QB = 256

epsilon = 1e-06
LOG2E = 1.4426950408889634
score_scale = LOG2E / 12.0

NT_DIMS = (((1,), (1,)), ((), ()))
TN_DIMS = (((0,), (0,)), ((), ()))


def iota(shape, dim):
    return lax.broadcasted_iota(jnp.int32, shape, dim)


def one_hot(mask):
    return jnp.where(mask, 1.0, 0.0).astype(BF16)


def mm(a, b, dims=None):
    if dims is None:
        return jnp.dot(a, b, preferred_element_type=F32)
    return lax.dot_general(a, b, dims, preferred_element_type=F32)


def span(index, size):
    return pl.ds(pl.multiple_of(index * size, size), size)


def merge(left, right):
    n = left.shape[1]
    pair = jnp.concatenate([left.reshape(16, 8, n), right.reshape(16, 8, n)], axis=1)
    return pair.reshape(256, n).astype(BF16)


def layer_kernel(
    old_hbm, rows_ref, gains_ref, hid_ref, master_hbm, out_ref,
    old_f, old_b, s1, b1, s2, b3, w, wp, nrm, xg, acc, psend, precv, z_qkv,
    att, hg, of, ow, sc, part_f, ps, rh, rf, mx, mixed, hid_y, gains_y,
    load_sem, loc_sem, send_sem, recv_sem,
):
    y = lax.axis_index("section")
    d = lax.axis_index("dp")
    c = lax.rem(d, 2)
    chip = lax.div(d, 2)
    x = lax.rem(chip, 4)
    z = lax.div(chip, 4)
    me = y * 32 + d

    def at(zz, xx, cc, yy=y):
        return (lax.rem(yy + 4, 4), (lax.rem(zz + 4, 4) * 4 + lax.rem(xx + 4, 4)) * 2 + cc)

    partner = at(z, x, 1 - c)
    ids = {}
    sent = []

    def slot(key):
        return ids.setdefault(key, len(ids))

    def send(key, src, dst, dev):
        n = slot(key)
        copy = pltpu.make_async_remote_copy(
            src_ref=src, dst_ref=dst, send_sem=send_sem.at[n], recv_sem=recv_sem.at[n],
            device_id=dev, device_id_type=MESH,
        )
        copy.start()
        sent.append(copy)

    def receive(key, dst):
        n = slot(key)
        pltpu.make_async_remote_copy(
            src_ref=dst, dst_ref=dst, send_sem=send_sem.at[n], recv_sem=recv_sem.at[n],
            device_id=partner, device_id_type=MESH,
        ).wait_recv()

    local_count = [0]

    def local(src, dst):
        copy = pltpu.make_async_copy(src, dst, loc_sem.at[local_count[0]])
        local_count[0] += 1
        copy.start()
        return copy

    def load(i):
        at_rows = pl.ds(i * 128, 128)
        return pltpu.make_async_copy(old_hbm.at[at_rows], old_f.at[at_rows], load_sem.at[i])

    for i in range(3):
        load(i).start()

    barrier = pltpu.get_barrier_semaphore()
    greeted = [at(z + j, x, c, y + i) for i in range(4) for j in range(4) if i or j]
    greeted += [at(z, x, 1 - c)]
    for k in (1, 2, 3):
        greeted += [at(z, x + k, c), at(z, x + k, 1 - c), at(z, x + k, c, y + 1), at(z, x + k, c, y + 3)]
    for dev in greeted:
        pl.semaphore_signal(barrier, inc=1, device_id=dev, device_id_type=MESH)

    h = hid_ref[...].astype(F32)
    scale = lax.rsqrt(jnp.mean(h * h, axis=-1, keepdims=True) + epsilon)
    nrm[...] = (h * scale * gains_ref[0:1, :]).astype(BF16)
    pl.semaphore_wait(barrier, len(greeted))

    own_rows = pl.ds(pl.multiple_of(chip * 128 + c * 64, 64), 64)
    other_rows = pl.ds(pl.multiple_of(chip * 128 + (1 - c) * 64, 64), 64)
    send("norm", nrm.at[:, span(1 - c, HALF)], xg.at[own_rows], partner)
    own_copy = local(nrm.at[:, span(c, HALF)], xg.at[own_rows])

    def ag_place(colour, fk, sk, half):
        if colour == 0:
            cc = lax.rem(z + sk + 4, 4) * 4 + lax.rem(x + fk + 4, 4)
        else:
            cc = lax.rem(z + fk + 4, 4) * 4 + lax.rem(x + sk + 4, 4)
        if half is None:
            rows = pl.ds(pl.multiple_of(cc * 128, 128), 128)
        else:
            rows = pl.ds(pl.multiple_of(cc * 128 + half * 64, 64), 64)
        return xg.at[rows, pl.ds(colour * COLOR, COLOR)]

    def ag_send(colour, axis, step, fk, sk, half=None):
        along_x = (axis == "f") == (colour == 0)
        dev = at(z, x + step, c) if along_x else at(z + step, x, c)
        ref = ag_place(colour, fk, sk, half)
        send(("ag", colour, axis, step, fk % 4, sk % 4, half), ref, ref, dev)

    def ag_recv(colour, axis, step, fk, sk, half=None):
        key = ("ag", colour, axis, step, fk % 4, sk % 4, half)
        if axis == "f":
            fk = (fk - step) % 4
        else:
            sk = (sk - step) % 4
        receive(key, ag_place(colour, fk, sk, half))

    def part(step):
        return 0 if step == 1 else 1

    both = [(colour, step) for colour in (0, 1) for step in (1, -1)]

    def tiles(count, body, size=TILE):
        def one(j, carry):
            body(span(j, size))
            return carry

        lax.fori_loop(0, count, one, 0)

    own_copy.wait()
    receive("norm", xg.at[other_rows])
    for step in (1, -1):
        ag_send(0, "f", step, 0, 0)
    for step in (1, -1):
        ag_send(1, "s", step, 0, 0)

    rows = rows_ref[...].reshape(1, SLAB)
    owner = jnp.floor((rows.astype(F32) + 0.5) * (1.0 / SLAB)).astype(jnp.int32)
    place = rows - owner * SLAB
    dest = iota((DEVICES, SLAB), 0)
    choose = one_hot((owner == dest) & (dest != me))
    keep_t = one_hot((rows - me * SLAB) == iota((SLAB, SLAB), 0))
    low_t = one_hot((place & 127) == iota((128, SLAB), 0))
    high_t = one_hot((place >> 7) == iota((128, SLAB), 0))
    for i in range(3):
        load(i).wait()

        def cast(j, carry):
            at_rows = pl.ds(pl.multiple_of(i * 128 + j * 16, 16), 16)
            old_b[at_rows, :] = old_f[at_rows, :].astype(BF16)
            return carry

        lax.fori_loop(0, 8, cast, 0)

    def choose_rows(j, carry):
        cols = span(j, TILE)
        cols2 = pl.ds(pl.multiple_of(HALF + j * TILE, TILE), TILE)
        s1[:, cols] = merge(mm(choose, old_b[:, cols]), mm(choose, old_b[:, cols2]))
        return carry

    lax.fori_loop(0, HALF // TILE, choose_rows, 0)
    s1[:, HALF:] = merge(mm(choose, low_t, NT_DIMS), mm(choose, high_t, NT_DIMS))

    group_me = y * 4 + z
    across = [(i, j) for i in (2, 1, 3, 0) for j in (2, 1, 3, 0) if i or j]
    for i, j in across:
        g = lax.rem(y + i, 4) * 4 + lax.rem(z + j, 4)
        send(("yz", i, j), s1.at[span(g, 16)], b1.at[span(group_me, 16)], at(z + j, x, c, y + i))
    own_yz = local(s1.at[span(group_me, 16)], b1.at[span(group_me, 16)])

    send("hid", hid_ref, hid_y, at(z, x, c, y + 1))
    send("gains", gains_ref, gains_y, at(z, x, c, y + 1))

    def keep_rows(cols):
        high = old_b[:, cols]
        rest = old_f[:, cols] - high.astype(F32)
        mid = rest.astype(BF16)
        low = (rest - mid.astype(F32)).astype(BF16)
        old_f[:, cols] = (mm(keep_t, high) + mm(keep_t, mid)) + mm(keep_t, low)

    def clear(j, carry):
        acc[span(j, 64), :] = jnp.zeros((64, 512), F32)
        return carry

    lax.fori_loop(0, TOK // 64, clear, 0)

    lax.fori_loop(0, 4, lambda j, t: (keep_rows(span(j, TILE)), t)[1], 0)

    for step in (1, -1):
        ag_recv(0, "f", step, 0, 0)
        ag_send(0, "f", step, -step, 0, part(step))

    own_yz.wait()
    for i, j in across:
        g = lax.rem(y + 4 - i, 4) * 4 + lax.rem(z + 4 - j, 4)
        receive(("yz", i, j), b1.at[span(g, 16)])

    for step in (1, -1):
        ag_send(1, "f", step, 0, 0)
    for fk in (0, -1, 1):
        for step in (1, -1):
            ag_send(0, "s", step, fk, 0)

    r2 = iota((DEVICES, 256), 0)
    from_row = (r2 & 15) * 16 + (r2 >> 4)
    perm_l = one_hot(iota((DEVICES, 256), 1) == from_row)
    perm_r = one_hot(iota((DEVICES, 256), 1) == from_row + 8)

    def regroup(j, carry):
        cols = span(j, TILE)
        cols2 = pl.ds(pl.multiple_of(HALF + j * TILE, TILE), TILE)
        piece = b1[:, cols]
        s2[:, cols] = mm(perm_l, piece).astype(BF16)
        s2[:, cols2] = mm(perm_r, piece).astype(BF16)
        return carry

    lax.fori_loop(0, HALF // TILE, regroup, 0)
    s2[:, D : D + 128] = mm(perm_l, b1[:, HALF:]).astype(BF16)
    s2[:, D + 128 :] = mm(perm_r, b1[:, HALF:]).astype(BF16)

    e_me = x * 2 + c
    for m in (4, 3, 5, 2, 6, 1, 7):
        e = lax.rem(e_me + m, 8)
        send(("xc", m), s2.at[span(e, 16)], b3.at[span(e_me, 16)], at(z, lax.div(e, 2), lax.rem(e, 2)))
    own_xc = local(s2.at[span(e_me, 16)], b3.at[span(e_me, 16)])

    for step in (1, -1):
        ag_recv(0, "f", step, -step, 0, part(step))
    for step in (1, -1):
        ag_send(0, "s", step, 2, 0)

    lax.fori_loop(4, D // TILE, lambda j, t: (keep_rows(span(j, TILE)), t)[1], 0)

    for step in (1, -1):
        ag_recv(1, "f", step, 0, 0)
        ag_send(1, "f", step, -step, 0, part(step))
    for step in (1, -1):
        ag_recv(1, "s", step, 0, 0)

    own_xc.wait()
    for m in (4, 3, 5, 2, 6, 1, 7):
        receive(("xc", m), b3.at[span(lax.rem(e_me + 8 - m, 8), 16)])

    for step in (1, -1):
        ag_send(1, "s", step, 0, -step, part(step))
    for fk in (-1, 1):
        for step in (1, -1):
            ag_send(1, "s", step, fk, 0)
    for step in (1, -1):
        ag_recv(0, "s", step, 0, 0)
        ag_send(0, "s", step, 0, -step, part(step))

    low_lab = b3[:, D : D + 128]
    high_lab = b3[:, D + 128 :]
    arrived = jnp.concatenate([low_lab * high_lab[:, a : a + 1] for a in range(3)], axis=1)

    def place_rows(cols):
        m = old_f[:, cols] + mm(arrived, b3[:, cols], TN_DIMS)
        old_f[:, cols] = m
        w[:, cols] = m.astype(BF16)

    tiles(D // TILE, place_rows)
    master_copy = local(old_f, master_hbm)

    theirs = span(1 - c, HALF)
    ours = span(c, HALF)
    k_rows = pl.ds(pl.multiple_of(256 + 64 * c, 64), 64)
    v_rows = pl.ds(pl.multiple_of(384 + 64 * c, 64), 64)
    k_rows_p = pl.ds(pl.multiple_of(256 + 64 * (1 - c), 64), 64)
    v_rows_p = pl.ds(pl.multiple_of(384 + 64 * (1 - c), 64), 64)
    o_rows = span(c, 128)
    o_rows_p = span(1 - c, 128)
    send("wq", w.at[0:128, theirs], wp.at[128:256], partner)
    send("wk", w.at[128:192, theirs], wp.at[k_rows], partner)
    send("wv", w.at[192:256, theirs], wp.at[v_rows], partner)
    send("wo", w.at[256:384], of.at[o_rows], partner)
    own_w = [
        local(w.at[0:128, ours], wp.at[0:128]),
        local(w.at[128:192, ours], wp.at[k_rows]),
        local(w.at[192:256, ours], wp.at[v_rows]),
        local(w.at[256:384], of.at[o_rows]),
    ]

    for step in (1, -1):
        ag_recv(1, "f", step, -step, 0, part(step))
    for step in (1, -1):
        ag_send(1, "s", step, 2, 0)
    for fk in (-1, 1):
        for colour in (0, 1):
            for step in (1, -1):
                ag_recv(colour, "s", step, fk, 0)
                ag_send(colour, "s", step, fk, -step, part(step))

    for copy in own_w:
        copy.wait()
    receive("wq", wp.at[128:256])
    receive("wk", wp.at[k_rows_p])
    receive("wv", wp.at[v_rows_p])
    receive("wo", of.at[o_rows_p])

    fi = x + c * (z - x)
    si = z + c * (x - z)

    def along_f(k, yy=y):
        return at(z + c * k, x + (1 - c) * k, c, yy)

    def along_s(k):
        return at(z + (1 - c) * k, x + c * k, c)

    def project(colour, fk):
        if colour == 0:
            xx = lax.rem(x + fk + 4, 4)
            places = [pl.ds(pl.multiple_of((q * 4 + xx) * 128, 128), 128) for q in range(4)]
        else:
            zz = lax.rem(z + fk + 4, 4)
            places = [pl.ds(pl.multiple_of((zz * 4 + q) * 128, 128), 128) for q in range(4)]
        cols = slice(colour * COLOR, (colour + 1) * COLOR)
        block = jnp.concatenate([xg[p, cols] for p in places], axis=0)
        out = mm(block, wp[:, cols], NT_DIMS)
        for q, p in enumerate(places):
            piece = out[q * 128 : (q + 1) * 128]
            acc[p, :] = acc[p, :] + piece

    def tokens_of(fk):
        for colour in (0, 1):
            for step in (1, -1):
                ag_recv(colour, "s", step, fk, -step, part(step))

    tokens_of(0)
    project(0, 0)
    project(1, 0)
    for colour, step in both:
        ag_recv(colour, "s", step, 2, 0)
        ag_send(colour, "s", step, 2, -step, part(step))
    tokens_of(-1)
    project(0, -1)
    project(1, -1)
    tokens_of(1)
    project(0, 1)
    project(1, 1)
    tokens_of(2)
    for k in (2, 1, 3):
        send(("ow", k), of.at[:, span(lax.rem(fi + k, 4), QUARTER)], ow.at[fi], along_f(k))
    own_o = local(of.at[:, span(fi, QUARTER)], ow.at[fi])
    project(0, 2)
    project(1, 2)

    for g in range(4):
        at_rows = pl.ds(g * GROUP, GROUP)
        psend[at_rows, :] = acc[at_rows, 128:512].astype(BF16)
        send(("proj", g), psend.at[at_rows], precv.at[at_rows], partner)

    def combine(g):
        at_rows = pl.ds(g * GROUP, GROUP)
        receive(("proj", g), precv.at[at_rows])
        q = acc[at_rows, 0:128] + precv[at_rows, 0:128].astype(F32)
        kv = acc[at_rows, 256:512] + precv[at_rows, 128:384].astype(F32)
        z_qkv[at_rows, 0:128] = q.astype(BF16)
        z_qkv[at_rows, 128:384] = kv.astype(BF16)

    def attend(qb):
        q = z_qkv[qb * QB : (qb + 1) * QB, 0:128]
        peak = None
        for kb in range(qb + 1):
            cols = slice(kb * QB, (kb + 1) * QB)
            s = mm(q, z_qkv[cols, 128:256], NT_DIMS) * score_scale
            if kb == qb:
                s = jnp.where(iota((QB, QB), 0) >= iota((QB, QB), 1), s, -1e30)
            sc[:, cols] = s
            top = jnp.maximum(s[:, 0:128], s[:, 128:256])
            peak = top if peak is None else jnp.maximum(peak, top)
        peak = jnp.max(peak, axis=-1, keepdims=True)
        total = None
        out = None
        for kb in range(qb + 1):
            cols = slice(kb * QB, (kb + 1) * QB)
            e = jnp.exp2(sc[:, cols] - peak)
            add = e[:, 0:128] + e[:, 128:256]
            total = add if total is None else total + add
            o = mm(e.astype(BF16), z_qkv[cols, 256:384])
            out = o if out is None else out + o
        total = jnp.sum(total, axis=-1, keepdims=True)
        out = (out / total).astype(BF16)
        for i in range(QB // 128):
            ci = qb * (QB // 128) + i
            att[0, ci * 64 : ci * 64 + 64, :] = out[i * 128 : i * 128 + 64]
            att[1, ci * 64 : ci * 64 + 64, :] = out[i * 128 + 64 : i * 128 + 128]

    head_cols = span(c, 128)
    head_cols_p = span(1 - c, 128)
    own_a = {}

    def f_at(k):
        return lax.rem(fi + k + 4, 4)

    def rows_g(g, half=None):
        return pl.ds(g * 256, 256) if half is None else pl.ds(g * 256 + half * 128, 128)

    def gather_1(g):
        send(("att", g), att.at[1 - c, rows_g(g)], hg.at[si, rows_g(g), head_cols], partner)
        own_a[g] = local(att.at[c, rows_g(g)], hg.at[fi, rows_g(g), head_cols])

    def gather_2(g):
        own_a[g].wait()
        receive(("att", g), hg.at[fi, rows_g(g), head_cols_p])
        for step in (1, -1):
            ref = hg.at[fi, rows_g(g)]
            send(("hg", step, g), ref, ref, along_f(step))

    def gather_3(g):
        for step in (1, -1):
            receive(("hg", step, g), hg.at[f_at(-step), rows_g(g)])
            ref = hg.at[f_at(-step), rows_g(g, part(step))]
            send(("hg2", step, g), ref, ref, along_f(step))

    combine(0)
    attend(0)
    attend(1)
    gather_1(0)
    combine(1)
    attend(2)
    gather_2(0)
    attend(3)
    gather_1(1)
    gather_3(0)
    combine(2)
    attend(4)
    gather_2(1)
    attend(5)
    gather_1(2)
    gather_3(1)
    combine(3)
    attend(6)
    gather_2(2)
    attend(7)
    gather_1(3)
    gather_3(2)
    gather_2(3)

    def products(g):
        for step in (1, -1):
            receive(("hg2", step, g), hg.at[f_at(2), rows_g(g, part(step))])

        def columns(cols):
            out = None
            for f in range(4):
                o = mm(hg[f, rows_g(g), :], ow[f, :, cols])
                out = o if out is None else out + o
            part_f[rows_g(g), cols] = out

        tiles(QUARTER // TILE, columns)

    own_o.wait()
    for k in (1, 3, 2):
        receive(("ow", k), ow.at[lax.rem(fi + 4 - k, 4)])
    products(0)
    gather_3(3)
    products(1)
    products(2)
    products(3)

    def source(j, k, half=None):
        s_there = lax.rem(si + j + 4, 4)
        first = s_there * (256 - 192 * c) + f_at(k) * (64 + 192 * c)
        if half is None:
            return pl.ds(pl.multiple_of(first, 64), 64)
        return pl.ds(pl.multiple_of(first + half * 32, 32), 32)

    order = (2, 1, 3, 0)

    def piece(k, half=None):
        q = f_at(k)
        if half is None:
            return pl.ds(pl.multiple_of(q * 64, 64), 64)
        return pl.ds(pl.multiple_of(q * 64 + half * 32, 32), 32)

    for k in order:
        ps[0, piece(k), :] = part_f[source(2, k), :].astype(BF16)
        for step in (1, -1):
            rows_k = piece(k, part(step))
            send(("rh", step, k), ps.at[0, rows_k], rh.at[part(step), rows_k], along_s(step))

    for k in order:
        for step in (1, -1):
            h_in = part(step)
            mine = piece(k, h_in)
            rest = piece(k, 1 - h_in)
            n = 1 + h_in
            ps[n, rest, :] = part_f[source(step, k, 1 - h_in), :].astype(BF16)
            receive(("rh", step, k), rh.at[h_in, mine])
            ps[n, mine, :] = (part_f[source(step, k, h_in), :] + rh[h_in, mine, :].astype(F32)).astype(BF16)
            send(("rf", step, k), ps.at[n, piece(k)], rf.at[h_in, piece(k)], along_s(step))

    for k in order:
        rows_k = piece(k)
        for step in (1, -1):
            receive(("rf", step, k), rf.at[part(step), rows_k])
        total = part_f[source(0, k), :] + rf[0, rows_k, :].astype(F32) + rf[1, rows_k, :].astype(F32)
        mx[rows_k, :] = total.astype(BF16)
        send(("mx", k), mx.at[rows_k], mixed.at[:, span(fi, QUARTER)], along_f(k, y + 1))

    receive("hid", hid_y)
    receive("gains", gains_y)
    for k in order:
        receive(("mx", k), mixed.at[:, span(lax.rem(fi + 4 - k, 4), QUARTER)])

    m = mixed[...].astype(F32)
    scale2 = lax.rsqrt(jnp.mean(m * m, axis=-1, keepdims=True) + epsilon)
    out_ref[...] = (hid_y[...].astype(F32) + m * scale2 * gains_y[1:2, :]).astype(BF16)

    master_copy.wait()
    for copy in sent:
        copy.wait_send()


def layer(old_master, rows, gains, hidden):
    vmem = pl.BlockSpec(memory_space=pltpu.VMEM)
    anywhere = pl.BlockSpec(memory_space=pl.ANY)
    return pl.pallas_call(
        layer_kernel,
        out_shape=(
            jax.ShapeDtypeStruct((SLAB, D), F32),
            jax.ShapeDtypeStruct((OWN_TOK, D), BF16),
        ),
        in_specs=[anywhere, vmem, vmem, vmem],
        out_specs=(anywhere, vmem),
        scratch_shapes=[
            pltpu.VMEM((SLAB, D), F32),
            pltpu.VMEM((SLAB, D), BF16),
            pltpu.VMEM((256, PIECE), BF16),
            pltpu.VMEM((256, PIECE), BF16),
            pltpu.VMEM((DEVICES, 2 * PIECE), BF16),
            pltpu.VMEM((DEVICES, 2 * PIECE), BF16),
            pltpu.VMEM((SLAB, D), BF16),
            pltpu.VMEM((512, HALF), BF16),
            pltpu.VMEM((OWN_TOK, D), BF16),
            pltpu.VMEM((TOK, HALF), BF16),
            pltpu.VMEM((TOK, 512), F32),
            pltpu.VMEM((TOK, 384), BF16),
            pltpu.VMEM((TOK, 384), BF16),
            pltpu.VMEM((TOK, 384), BF16),
            pltpu.VMEM((2, TOK // 2, 128), BF16),
            pltpu.VMEM((4, TOK // 2, 256), BF16),
            pltpu.VMEM((256, D), BF16),
            pltpu.VMEM((4, 256, QUARTER), BF16),
            pltpu.VMEM((QB, TOK), F32),
            pltpu.VMEM((TOK // 2, QUARTER), F32),
            pltpu.VMEM((3, 256, QUARTER), BF16),
            pltpu.VMEM((2, 256, QUARTER), BF16),
            pltpu.VMEM((2, 256, QUARTER), BF16),
            pltpu.VMEM((256, QUARTER), BF16),
            pltpu.VMEM((OWN_TOK, D), BF16),
            pltpu.VMEM((OWN_TOK, D), BF16),
            pltpu.VMEM((2, D), F32),
            pltpu.SemaphoreType.DMA((3,)),
            pltpu.SemaphoreType.DMA((16,)),
            pltpu.SemaphoreType.DMA((128,)),
            pltpu.SemaphoreType.DMA((128,)),
        ],
        compiler_params=pltpu.CompilerParams(
            collective_id=0, has_side_effects=True, vmem_limit_bytes=63 * 1024 * 1024
        ),
    )(old_master, rows, gains, hidden)


def body(old_master, old_rows, gains, hidden_in):
    master, hidden_out = layer(old_master, old_rows, gains[0], hidden_in[0])
    return (master, hidden_out[None])


def solution(mesh):
    in_specs = (
        P(("section", "dp"), None),
        P(("section", "dp")),
        P("section", None, None),
        P("section", "dp", None),
    )
    out_specs = (P(("section", "dp"), None), P("section", "dp", None))
    return jax.shard_map(body, mesh=mesh, in_specs=in_specs, out_specs=out_specs, check_vma=False)
```

```python
import jax
import jax.numpy as jnp
from jax import lax
from jax.experimental import pallas as pl
from jax.experimental.pallas import tpu as pltpu
from jax.sharding import PartitionSpec as P

MESH = pl.DeviceIdType.MESH
F32 = jnp.float32
BF16 = jnp.bfloat16

D = 4608
HD = 128
SLAB = 384
TOK = 2048
OWN_TOK = 64
HALF = D // 2
COLOR = HALF // 2
QUARTER = D // 4
DEVICES = 128
PIECE = HALF + 128
TILE = 384
GROUP = 512
QB = 256

epsilon = 1e-06
LOG2E = 1.4426950408889634
score_scale = LOG2E / 12.0

NT_DIMS = (((1,), (1,)), ((), ()))
TN_DIMS = (((0,), (0,)), ((), ()))


def iota(shape, dim):
    return lax.broadcasted_iota(jnp.int32, shape, dim)


def one_hot(mask):
    return jnp.where(mask, 1.0, 0.0).astype(BF16)


def mm(a, b, dims=None):
    if dims is None:
        return jnp.dot(a, b, preferred_element_type=F32)
    return lax.dot_general(a, b, dims, preferred_element_type=F32)


def span(index, size):
    return pl.ds(pl.multiple_of(index * size, size), size)


def merge(left, right):
    n = left.shape[1]
    pair = jnp.concatenate([left.reshape(16, 8, n), right.reshape(16, 8, n)], axis=1)
    return pair.reshape(256, n).astype(BF16)


def layer_kernel(
    old_hbm, rows_ref, gains_ref, hid_ref, master_hbm, out_ref,
    old_f, old_b, s1, b1, s2, b3, w, wp, nrm, xg, acc, psend, precv, z_qkv,
    att, hg, of, ow, sc, part_f, ps, rh, rf, mx, mixed, hid_y, gains_y,
    load_sem, loc_sem, send_sem, recv_sem,
):
    y = lax.axis_index("section")
    d = lax.axis_index("dp")
    c = lax.rem(d, 2)
    chip = lax.div(d, 2)
    x = lax.rem(chip, 4)
    z = lax.div(chip, 4)
    me = y * 32 + d

    def at(zz, xx, cc, yy=y):
        return (lax.rem(yy + 4, 4), (lax.rem(zz + 4, 4) * 4 + lax.rem(xx + 4, 4)) * 2 + cc)

    partner = at(z, x, 1 - c)
    ids = {}
    sent = []

    def slot(key):
        return ids.setdefault(key, len(ids))

    def send(key, src, dst, dev):
        n = slot(key)
        copy = pltpu.make_async_remote_copy(
            src_ref=src, dst_ref=dst, send_sem=send_sem.at[n], recv_sem=recv_sem.at[n],
            device_id=dev, device_id_type=MESH,
        )
        copy.start()
        sent.append(copy)

    def receive(key, dst):
        n = slot(key)
        pltpu.make_async_remote_copy(
            src_ref=dst, dst_ref=dst, send_sem=send_sem.at[n], recv_sem=recv_sem.at[n],
            device_id=partner, device_id_type=MESH,
        ).wait_recv()

    local_count = [0]

    def local(src, dst):
        copy = pltpu.make_async_copy(src, dst, loc_sem.at[local_count[0]])
        local_count[0] += 1
        copy.start()
        return copy

    def load(i):
        at_rows = pl.ds(i * 128, 128)
        return pltpu.make_async_copy(old_hbm.at[at_rows], old_f.at[at_rows], load_sem.at[i])

    for i in range(3):
        load(i).start()

    barrier = pltpu.get_barrier_semaphore()
    greeted = [at(z + j, x, c, y + i) for i in range(4) for j in range(4) if i or j]
    greeted += [at(z, x, 1 - c)]
    for k in (1, 2, 3):
        greeted += [at(z, x + k, c), at(z, x + k, 1 - c), at(z, x + k, c, y + 1), at(z, x + k, c, y + 3)]
    for dev in greeted:
        pl.semaphore_signal(barrier, inc=1, device_id=dev, device_id_type=MESH)

    h = hid_ref[...].astype(F32)
    scale = lax.rsqrt(jnp.mean(h * h, axis=-1, keepdims=True) + epsilon)
    nrm[...] = (h * scale * gains_ref[0:1, :]).astype(BF16)
    pl.semaphore_wait(barrier, len(greeted))

    own_rows = pl.ds(pl.multiple_of(chip * 128 + c * 64, 64), 64)
    other_rows = pl.ds(pl.multiple_of(chip * 128 + (1 - c) * 64, 64), 64)
    send("norm", nrm.at[:, span(1 - c, HALF)], xg.at[own_rows], partner)
    own_copy = local(nrm.at[:, span(c, HALF)], xg.at[own_rows])

    def ag_place(colour, fk, sk, half):
        if colour == 0:
            cc = lax.rem(z + sk + 4, 4) * 4 + lax.rem(x + fk + 4, 4)
        else:
            cc = lax.rem(z + fk + 4, 4) * 4 + lax.rem(x + sk + 4, 4)
        if half is None:
            rows = pl.ds(pl.multiple_of(cc * 128, 128), 128)
        else:
            rows = pl.ds(pl.multiple_of(cc * 128 + half * 64, 64), 64)
        return xg.at[rows, pl.ds(colour * COLOR, COLOR)]

    def ag_send(colour, axis, step, fk, sk, half=None):
        along_x = (axis == "f") == (colour == 0)
        dev = at(z, x + step, c) if along_x else at(z + step, x, c)
        ref = ag_place(colour, fk, sk, half)
        send(("ag", colour, axis, step, fk % 4, sk % 4, half), ref, ref, dev)

    def ag_recv(colour, axis, step, fk, sk, half=None):
        key = ("ag", colour, axis, step, fk % 4, sk % 4, half)
        if axis == "f":
            fk = (fk - step) % 4
        else:
            sk = (sk - step) % 4
        receive(key, ag_place(colour, fk, sk, half))

    def part(step):
        return 0 if step == 1 else 1

    both = [(colour, step) for colour in (0, 1) for step in (1, -1)]

    def tiles(count, body, size=TILE):
        def one(j, carry):
            body(span(j, size))
            return carry

        lax.fori_loop(0, count, one, 0)

    own_copy.wait()
    receive("norm", xg.at[other_rows])
    for colour, step in both:
        ag_send(colour, "f", step, 0, 0)
    for colour, step in both:
        ag_send(colour, "s", step, 0, 0)

    rows = rows_ref[...].reshape(1, SLAB)
    owner = jnp.floor((rows.astype(F32) + 0.5) * (1.0 / SLAB)).astype(jnp.int32)
    place = rows - owner * SLAB
    dest = iota((DEVICES, SLAB), 0)
    choose = one_hot((owner == dest) & (dest != me))
    keep_t = one_hot((rows - me * SLAB) == iota((SLAB, SLAB), 0))
    low_t = one_hot((place & 127) == iota((128, SLAB), 0))
    high_t = one_hot((place >> 7) == iota((128, SLAB), 0))
    for i in range(3):
        load(i).wait()

        def cast(j, carry):
            at_rows = pl.ds(pl.multiple_of(i * 128 + j * 16, 16), 16)
            old_b[at_rows, :] = old_f[at_rows, :].astype(BF16)
            return carry

        lax.fori_loop(0, 8, cast, 0)

    def choose_rows(j, carry):
        cols = span(j, TILE)
        cols2 = pl.ds(pl.multiple_of(HALF + j * TILE, TILE), TILE)
        s1[:, cols] = merge(mm(choose, old_b[:, cols]), mm(choose, old_b[:, cols2]))
        return carry

    lax.fori_loop(0, HALF // TILE, choose_rows, 0)
    s1[:, HALF:] = merge(mm(choose, low_t, NT_DIMS), mm(choose, high_t, NT_DIMS))

    group_me = y * 4 + z
    across = [(i, j) for i in (2, 1, 3, 0) for j in (2, 1, 3, 0) if i or j]
    for i, j in across:
        g = lax.rem(y + i, 4) * 4 + lax.rem(z + j, 4)
        send(("yz", i, j), s1.at[span(g, 16)], b1.at[span(group_me, 16)], at(z + j, x, c, y + i))
    own_yz = local(s1.at[span(group_me, 16)], b1.at[span(group_me, 16)])

    def keep_rows(cols):
        high = old_b[:, cols]
        rest = old_f[:, cols] - high.astype(F32)
        mid = rest.astype(BF16)
        low = (rest - mid.astype(F32)).astype(BF16)
        old_f[:, cols] = (mm(keep_t, high) + mm(keep_t, mid)) + mm(keep_t, low)

    lax.fori_loop(0, 6, lambda j, t: (keep_rows(span(j, TILE)), t)[1], 0)

    for colour, step in both:
        ag_recv(colour, "f", step, 0, 0)
        ag_send(colour, "f", step, -step, 0, part(step))
        for step2 in (1, -1):
            ag_send(colour, "s", step2, -step, 0)
    for colour, step in both:
        ag_recv(colour, "s", step, 0, 0)
        ag_send(colour, "s", step, 0, -step, part(step))

    lax.fori_loop(6, D // TILE, lambda j, t: (keep_rows(span(j, TILE)), t)[1], 0)

    own_yz.wait()
    for i, j in across:
        g = lax.rem(y + 4 - i, 4) * 4 + lax.rem(z + 4 - j, 4)
        receive(("yz", i, j), b1.at[span(g, 16)])

    r2 = iota((DEVICES, 256), 0)
    from_row = (r2 & 15) * 16 + (r2 >> 4)
    perm_l = one_hot(iota((DEVICES, 256), 1) == from_row)
    perm_r = one_hot(iota((DEVICES, 256), 1) == from_row + 8)

    def regroup(j, carry):
        cols = span(j, TILE)
        cols2 = pl.ds(pl.multiple_of(HALF + j * TILE, TILE), TILE)
        piece = b1[:, cols]
        s2[:, cols] = mm(perm_l, piece).astype(BF16)
        s2[:, cols2] = mm(perm_r, piece).astype(BF16)
        return carry

    lax.fori_loop(0, HALF // TILE, regroup, 0)
    s2[:, D : D + 128] = mm(perm_l, b1[:, HALF:]).astype(BF16)
    s2[:, D + 128 :] = mm(perm_r, b1[:, HALF:]).astype(BF16)

    e_me = x * 2 + c
    for m in (4, 3, 5, 2, 6, 1, 7):
        e = lax.rem(e_me + m, 8)
        send(("xc", m), s2.at[span(e, 16)], b3.at[span(e_me, 16)], at(z, lax.div(e, 2), lax.rem(e, 2)))
    own_xc = local(s2.at[span(e_me, 16)], b3.at[span(e_me, 16)])

    send("hid", hid_ref, hid_y, at(z, x, c, y + 1))
    send("gains", gains_ref, gains_y, at(z, x, c, y + 1))

    for colour in (0, 1):
        for step in (1, -1):
            ag_recv(colour, "f", step, -step, 0, part(step))
        for step in (1, -1):
            ag_send(colour, "s", step, 2, 0)
    for fk in (-1, 1):
        for colour, step in both:
            ag_recv(colour, "s", step, fk, 0)
            ag_send(colour, "s", step, fk, -step, part(step))

    own_xc.wait()
    for m in (4, 3, 5, 2, 6, 1, 7):
        receive(("xc", m), b3.at[span(lax.rem(e_me + 8 - m, 8), 16)])

    low_lab = b3[:, D : D + 128]
    high_lab = b3[:, D + 128 :]
    arrived = jnp.concatenate([low_lab * high_lab[:, a : a + 1] for a in range(3)], axis=1)

    def place_rows(cols):
        m = old_f[:, cols] + mm(arrived, b3[:, cols], TN_DIMS)
        old_f[:, cols] = m
        w[:, cols] = m.astype(BF16)

    tiles(D // TILE, place_rows)
    master_copy = local(old_f, master_hbm)

    theirs = span(1 - c, HALF)
    ours = span(c, HALF)
    k_rows = pl.ds(pl.multiple_of(256 + 64 * c, 64), 64)
    v_rows = pl.ds(pl.multiple_of(384 + 64 * c, 64), 64)
    k_rows_p = pl.ds(pl.multiple_of(256 + 64 * (1 - c), 64), 64)
    v_rows_p = pl.ds(pl.multiple_of(384 + 64 * (1 - c), 64), 64)
    o_rows = span(c, 128)
    o_rows_p = span(1 - c, 128)
    send("wq", w.at[0:128, theirs], wp.at[128:256], partner)
    send("wk", w.at[128:192, theirs], wp.at[k_rows], partner)
    send("wv", w.at[192:256, theirs], wp.at[v_rows], partner)
    send("wo", w.at[256:384], of.at[o_rows], partner)
    own_w = [
        local(w.at[0:128, ours], wp.at[0:128]),
        local(w.at[128:192, ours], wp.at[k_rows]),
        local(w.at[192:256, ours], wp.at[v_rows]),
        local(w.at[256:384], of.at[o_rows]),
    ]

    for colour, step in both:
        ag_recv(colour, "s", step, 2, 0)
        ag_send(colour, "s", step, 2, -step, part(step))

    for copy in own_w:
        copy.wait()
    receive("wq", wp.at[128:256])
    receive("wk", wp.at[k_rows_p])
    receive("wv", wp.at[v_rows_p])
    receive("wo", of.at[o_rows_p])

    fi = x + c * (z - x)
    si = z + c * (x - z)

    def along_f(k, yy=y):
        return at(z + c * k, x + (1 - c) * k, c, yy)

    def along_s(k):
        return at(z + (1 - c) * k, x + c * k, c)

    for k in (2, 1, 3):
        send(("ow", k), of.at[:, span(lax.rem(fi + k, 4), QUARTER)], ow.at[fi], along_f(k))
    own_o = local(of.at[:, span(fi, QUARTER)], ow.at[fi])

    def project(colour, fk, fresh):
        if colour == 0:
            xx = lax.rem(x + fk + 4, 4)
            places = [pl.ds(pl.multiple_of((q * 4 + xx) * 128, 128), 128) for q in range(4)]
        else:
            zz = lax.rem(z + fk + 4, 4)
            places = [pl.ds(pl.multiple_of((zz * 4 + q) * 128, 128), 128) for q in range(4)]
        cols = slice(colour * COLOR, (colour + 1) * COLOR)
        block = jnp.concatenate([xg[p, cols] for p in places], axis=0)
        out = mm(block, wp[:, cols], NT_DIMS)
        for q, p in enumerate(places):
            piece = out[q * 128 : (q + 1) * 128]
            acc[p, :] = piece if fresh else acc[p, :] + piece

    for colour in (0, 1):
        for fk in (0, -1, 1, 2):
            for step in (1, -1):
                ag_recv(colour, "s", step, fk, -step, part(step))
            project(colour, fk, colour == 0)

    for g in range(4):
        at_rows = pl.ds(g * GROUP, GROUP)
        psend[at_rows, :] = acc[at_rows, 128:512].astype(BF16)
        send(("proj", g), psend.at[at_rows], precv.at[at_rows], partner)

    def combine(g):
        at_rows = pl.ds(g * GROUP, GROUP)
        receive(("proj", g), precv.at[at_rows])
        q = acc[at_rows, 0:128] + precv[at_rows, 0:128].astype(F32)
        kv = acc[at_rows, 256:512] + precv[at_rows, 128:384].astype(F32)
        z_qkv[at_rows, 0:128] = q.astype(BF16)
        z_qkv[at_rows, 128:384] = kv.astype(BF16)

    def attend(qb):
        q = z_qkv[qb * QB : (qb + 1) * QB, 0:128]
        peak = None
        for kb in range(qb + 1):
            cols = slice(kb * QB, (kb + 1) * QB)
            s = mm(q, z_qkv[cols, 128:256], NT_DIMS) * score_scale
            if kb == qb:
                s = jnp.where(iota((QB, QB), 0) >= iota((QB, QB), 1), s, -1e30)
            sc[:, cols] = s
            top = jnp.maximum(s[:, 0:128], s[:, 128:256])
            peak = top if peak is None else jnp.maximum(peak, top)
        peak = jnp.max(peak, axis=-1, keepdims=True)
        total = None
        out = None
        for kb in range(qb + 1):
            cols = slice(kb * QB, (kb + 1) * QB)
            e = jnp.exp2(sc[:, cols] - peak)
            add = e[:, 0:128] + e[:, 128:256]
            total = add if total is None else total + add
            o = mm(e.astype(BF16), z_qkv[cols, 256:384])
            out = o if out is None else out + o
        total = jnp.sum(total, axis=-1, keepdims=True)
        out = (out / total).astype(BF16)
        for i in range(QB // 128):
            ci = qb * (QB // 128) + i
            for core in range(2):
                for half in range(2):
                    first = i * 128 + core * 64 + half * 32
                    at_row = half * 512 + ci * 32
                    att[core, at_row : at_row + 32, :] = out[first : first + 32]

    head_cols = span(c, 128)
    head_cols_p = span(1 - c, 128)
    own_a = {}

    def f_at(k):
        return lax.rem(fi + k + 4, 4)

    def rows_g(g, half=None):
        return pl.ds(g * 512, 512) if half is None else pl.ds(g * 512 + half * 256, 256)

    def gather_1(g):
        send(("att", g), att.at[1 - c, rows_g(g)], hg.at[si, rows_g(g), head_cols], partner)
        own_a[g] = local(att.at[c, rows_g(g)], hg.at[fi, rows_g(g), head_cols])

    def gather_2(g):
        own_a[g].wait()
        receive(("att", g), hg.at[fi, rows_g(g), head_cols_p])
        for step in (1, -1):
            ref = hg.at[fi, rows_g(g)]
            send(("hg", step, g), ref, ref, along_f(step))

    def gather_3(g):
        for step in (1, -1):
            receive(("hg", step, g), hg.at[f_at(-step), rows_g(g)])
            ref = hg.at[f_at(-step), rows_g(g, part(step))]
            send(("hg2", step, g), ref, ref, along_f(step))

    for g in range(4):
        combine(g)
        attend(2 * g)
        attend(2 * g + 1)

    def products(g):
        for step in (1, -1):
            receive(("hg2", step, g), hg.at[f_at(2), rows_g(g, part(step))])

        def columns(cols):
            out = None
            for f in range(4):
                o = mm(hg[f, rows_g(g), :], ow[f, :, cols])
                out = o if out is None else out + o
            part_f[rows_g(g), cols] = out

        tiles(QUARTER // TILE, columns)

    def source(j, q, g):
        s_there = lax.rem(si + j + 4, 4)
        block = s_there * (4 - 3 * c) + q * (1 + 3 * c)
        return pl.ds(pl.multiple_of(g * 512 + block * 32, 32), 32)

    def half_rows(g):
        return pl.ds(g * 64, 64)

    def all_rows(g):
        return pl.ds(g * 128, 128)

    def q_rows(g, q):
        return pl.ds(g * 128 + q * 32, 32)

    def reduce_1(g):
        for q in range(4):
            ps[0, q_rows(g, q), :] = part_f[source(2, q, g), :].astype(BF16)
        for step in (1, -1):
            src = ps.at[0, pl.ds(g * 128 + part(step) * 64, 64)]
            send(("rh", step, g), src, rh.at[part(step), half_rows(g)], along_s(step))

    def reduce_2(g):
        for step in (1, -1):
            h_in = part(step)
            n = 1 + h_in
            for q in range(4):
                if q // 2 != h_in:
                    ps[n, q_rows(g, q), :] = part_f[source(step, q, g), :].astype(BF16)
            receive(("rh", step, g), rh.at[h_in, half_rows(g)])
            for q in range(4):
                if q // 2 == h_in:
                    came = rh[h_in, pl.ds(g * 64 + (q % 2) * 32, 32), :].astype(F32)
                    ps[n, q_rows(g, q), :] = (part_f[source(step, q, g), :] + came).astype(BF16)
            send(("rf", step, g), ps.at[n, all_rows(g)], rf.at[h_in, all_rows(g)], along_s(step))

    order = (2, 1, 3, 0)

    def reduce_3(g):
        for step in (1, -1):
            receive(("rf", step, g), rf.at[part(step), all_rows(g)])
        for q in range(4):
            rows_q = q_rows(g, q)
            came = rf[0, rows_q, :].astype(F32) + rf[1, rows_q, :].astype(F32)
            mx[rows_q, :] = (part_f[source(0, q, g), :] + came).astype(BF16)
        for k in order:
            src = mx.at[pl.ds(pl.multiple_of(g * 128 + f_at(k) * 32, 32), 32)]
            send(("mx", k, g), src, mixed.at[pl.ds(g * 32, 32), span(fi, QUARTER)], along_f(k, y + 1))

    def finish(g):
        at_rows = pl.ds(g * 32, 32)
        for k in order:
            receive(("mx", k, g), mixed.at[at_rows, span(lax.rem(fi + 4 - k, 4), QUARTER)])
        m = mixed[at_rows, :].astype(F32)
        scale2 = lax.rsqrt(jnp.mean(m * m, axis=-1, keepdims=True) + epsilon)
        out_ref[at_rows, :] = (hid_y[at_rows, :].astype(F32) + m * scale2 * gains_y[1:2, :]).astype(BF16)

    gather_1(0)
    gather_1(1)
    gather_2(0)
    gather_3(0)
    gather_2(1)
    own_o.wait()
    for k in (1, 3, 2):
        receive(("ow", k), ow.at[lax.rem(fi + 4 - k, 4)])
    products(0)
    reduce_1(0)
    gather_3(1)
    reduce_2(0)
    products(1)
    reduce_1(1)
    reduce_3(0)
    reduce_2(1)
    reduce_3(1)
    receive("hid", hid_y)
    receive("gains", gains_y)
    finish(0)
    finish(1)

    master_copy.wait()
    for copy in sent:
        copy.wait_send()


def layer(old_master, rows, gains, hidden):
    vmem = pl.BlockSpec(memory_space=pltpu.VMEM)
    anywhere = pl.BlockSpec(memory_space=pl.ANY)
    return pl.pallas_call(
        layer_kernel,
        out_shape=(
            jax.ShapeDtypeStruct((SLAB, D), F32),
            jax.ShapeDtypeStruct((OWN_TOK, D), BF16),
        ),
        in_specs=[anywhere, vmem, vmem, vmem],
        out_specs=(anywhere, vmem),
        scratch_shapes=[
            pltpu.VMEM((SLAB, D), F32),
            pltpu.VMEM((SLAB, D), BF16),
            pltpu.VMEM((256, PIECE), BF16),
            pltpu.VMEM((256, PIECE), BF16),
            pltpu.VMEM((DEVICES, 2 * PIECE), BF16),
            pltpu.VMEM((DEVICES, 2 * PIECE), BF16),
            pltpu.VMEM((SLAB, D), BF16),
            pltpu.VMEM((512, HALF), BF16),
            pltpu.VMEM((OWN_TOK, D), BF16),
            pltpu.VMEM((TOK, HALF), BF16),
            pltpu.VMEM((TOK, 512), F32),
            pltpu.VMEM((TOK, 384), BF16),
            pltpu.VMEM((TOK, 384), BF16),
            pltpu.VMEM((TOK, 384), BF16),
            pltpu.VMEM((2, TOK // 2, 128), BF16),
            pltpu.VMEM((4, TOK // 2, 256), BF16),
            pltpu.VMEM((256, D), BF16),
            pltpu.VMEM((4, 256, QUARTER), BF16),
            pltpu.VMEM((QB, TOK), F32),
            pltpu.VMEM((TOK // 2, QUARTER), F32),
            pltpu.VMEM((3, 256, QUARTER), BF16),
            pltpu.VMEM((2, 128, QUARTER), BF16),
            pltpu.VMEM((2, 256, QUARTER), BF16),
            pltpu.VMEM((256, QUARTER), BF16),
            pltpu.VMEM((OWN_TOK, D), BF16),
            pltpu.VMEM((OWN_TOK, D), BF16),
            pltpu.VMEM((2, D), F32),
            pltpu.SemaphoreType.DMA((3,)),
            pltpu.SemaphoreType.DMA((16,)),
            pltpu.SemaphoreType.DMA((128,)),
            pltpu.SemaphoreType.DMA((128,)),
        ],
        compiler_params=pltpu.CompilerParams(
            collective_id=0, has_side_effects=True, vmem_limit_bytes=63 * 1024 * 1024
        ),
    )(old_master, rows, gains, hidden)


def body(old_master, old_rows, gains, hidden_in):
    master, hidden_out = layer(old_master, old_rows, gains[0], hidden_in[0])
    return (master, hidden_out[None])


def solution(mesh):
    in_specs = (
        P(("section", "dp"), None),
        P(("section", "dp")),
        P("section", None, None),
        P("section", "dp", None),
    )
    out_specs = (P(("section", "dp"), None), P("section", "dp", None))
    return jax.shard_map(body, mesh=mesh, in_specs=in_specs, out_specs=out_specs, check_vma=False)
```

```python
import jax
import jax.numpy as jnp
from jax import lax
from jax.experimental import pallas as pl
from jax.experimental.pallas import tpu as pltpu
from jax.sharding import PartitionSpec as P

MESH = pl.DeviceIdType.MESH
F32 = jnp.float32
BF16 = jnp.bfloat16

D = 4608
HD = 128
SLAB = 384
TOK = 2048
OWN_TOK = 64
HALF = D // 2
COLOR = HALF // 2
QUARTER = D // 4
DEVICES = 128
PIECE = HALF + 128
TILE = 384
GROUP = 512
QB = 256

epsilon = 1e-06
LOG2E = 1.4426950408889634
score_scale = LOG2E / 12.0

NT_DIMS = (((1,), (1,)), ((), ()))
TN_DIMS = (((0,), (0,)), ((), ()))


def iota(shape, dim):
    return lax.broadcasted_iota(jnp.int32, shape, dim)


def one_hot(mask):
    return jnp.where(mask, 1.0, 0.0).astype(BF16)


def mm(a, b, dims=None):
    if dims is None:
        return jnp.dot(a, b, preferred_element_type=F32)
    return lax.dot_general(a, b, dims, preferred_element_type=F32)


def span(index, size):
    return pl.ds(pl.multiple_of(index * size, size), size)


def merge(left, right):
    n = left.shape[1]
    pair = jnp.concatenate([left.reshape(16, 8, n), right.reshape(16, 8, n)], axis=1)
    return pair.reshape(256, n).astype(BF16)


def layer_kernel(
    old_hbm, rows_ref, gains_ref, hid_ref, master_hbm, out_ref,
    old_f, old_b, s1, b1, s2, b3, w, wp, nrm, xg, acc, psend, precv, z_qkv,
    att, hg, of, ow, sc, part_f, ps, rh, rf, mx, mixed, hid_y, gains_y,
    load_sem, loc_sem, send_sem, recv_sem,
):
    y = lax.axis_index("section")
    d = lax.axis_index("dp")
    c = lax.rem(d, 2)
    chip = lax.div(d, 2)
    x = lax.rem(chip, 4)
    z = lax.div(chip, 4)
    me = y * 32 + d

    def at(zz, xx, cc, yy=y):
        return (lax.rem(yy + 4, 4), (lax.rem(zz + 4, 4) * 4 + lax.rem(xx + 4, 4)) * 2 + cc)

    partner = at(z, x, 1 - c)
    ids = {}
    sent = []

    def slot(key):
        return ids.setdefault(key, len(ids))

    def send(key, src, dst, dev):
        n = slot(key)
        copy = pltpu.make_async_remote_copy(
            src_ref=src, dst_ref=dst, send_sem=send_sem.at[n], recv_sem=recv_sem.at[n],
            device_id=dev, device_id_type=MESH,
        )
        copy.start()
        sent.append(copy)

    def receive(key, dst):
        n = slot(key)
        pltpu.make_async_remote_copy(
            src_ref=dst, dst_ref=dst, send_sem=send_sem.at[n], recv_sem=recv_sem.at[n],
            device_id=partner, device_id_type=MESH,
        ).wait_recv()

    local_count = [0]

    def local(src, dst):
        copy = pltpu.make_async_copy(src, dst, loc_sem.at[local_count[0]])
        local_count[0] += 1
        copy.start()
        return copy

    def load(i):
        at_rows = pl.ds(i * 128, 128)
        return pltpu.make_async_copy(old_hbm.at[at_rows], old_f.at[at_rows], load_sem.at[i])

    for i in range(3):
        load(i).start()

    barrier = pltpu.get_barrier_semaphore()
    greeted = [at(z + j, x, c, y + i) for i in range(4) for j in range(4) if i or j]
    greeted += [at(z, x, 1 - c)]
    for k in (1, 2, 3):
        greeted += [at(z, x + k, c), at(z, x + k, 1 - c), at(z, x + k, c, y + 1), at(z, x + k, c, y + 3)]
    for dev in greeted:
        pl.semaphore_signal(barrier, inc=1, device_id=dev, device_id_type=MESH)

    h = hid_ref[...].astype(F32)
    scale = lax.rsqrt(jnp.mean(h * h, axis=-1, keepdims=True) + epsilon)
    nrm[...] = (h * scale * gains_ref[0:1, :]).astype(BF16)
    pl.semaphore_wait(barrier, len(greeted))

    own_rows = pl.ds(pl.multiple_of(chip * 128 + c * 64, 64), 64)
    other_rows = pl.ds(pl.multiple_of(chip * 128 + (1 - c) * 64, 64), 64)
    send("norm", nrm.at[:, span(1 - c, HALF)], xg.at[own_rows], partner)
    own_copy = local(nrm.at[:, span(c, HALF)], xg.at[own_rows])

    def ag_place(colour, fk, sk, half):
        if colour == 0:
            cc = lax.rem(z + sk + 4, 4) * 4 + lax.rem(x + fk + 4, 4)
        else:
            cc = lax.rem(z + fk + 4, 4) * 4 + lax.rem(x + sk + 4, 4)
        if half is None:
            rows = pl.ds(pl.multiple_of(cc * 128, 128), 128)
        else:
            rows = pl.ds(pl.multiple_of(cc * 128 + half * 64, 64), 64)
        return xg.at[rows, pl.ds(colour * COLOR, COLOR)]

    def ag_send(colour, axis, step, fk, sk, half=None):
        along_x = (axis == "f") == (colour == 0)
        dev = at(z, x + step, c) if along_x else at(z + step, x, c)
        ref = ag_place(colour, fk, sk, half)
        send(("ag", colour, axis, step, fk % 4, sk % 4, half), ref, ref, dev)

    def ag_recv(colour, axis, step, fk, sk, half=None):
        key = ("ag", colour, axis, step, fk % 4, sk % 4, half)
        if axis == "f":
            fk = (fk - step) % 4
        else:
            sk = (sk - step) % 4
        receive(key, ag_place(colour, fk, sk, half))

    def part(step):
        return 0 if step == 1 else 1

    both = [(colour, step) for colour in (0, 1) for step in (1, -1)]

    def tiles(count, body, size=TILE):
        def one(j, carry):
            body(span(j, size))
            return carry

        lax.fori_loop(0, count, one, 0)

    own_copy.wait()
    receive("norm", xg.at[other_rows])
    for colour, step in both:
        ag_send(colour, "f", step, 0, 0)
    for colour, step in both:
        ag_send(colour, "s", step, 0, 0)

    rows = rows_ref[...].reshape(1, SLAB)
    owner = jnp.floor((rows.astype(F32) + 0.5) * (1.0 / SLAB)).astype(jnp.int32)
    place = rows - owner * SLAB
    dest = iota((DEVICES, SLAB), 0)
    choose = one_hot((owner == dest) & (dest != me))
    keep_t = one_hot((rows - me * SLAB) == iota((SLAB, SLAB), 0))
    low_t = one_hot((place & 127) == iota((128, SLAB), 0))
    high_t = one_hot((place >> 7) == iota((128, SLAB), 0))
    for i in range(3):
        load(i).wait()

        def cast(j, carry):
            at_rows = pl.ds(pl.multiple_of(i * 128 + j * 16, 16), 16)
            old_b[at_rows, :] = old_f[at_rows, :].astype(BF16)
            return carry

        lax.fori_loop(0, 8, cast, 0)

    def choose_rows(j, carry):
        cols = span(j, TILE)
        cols2 = pl.ds(pl.multiple_of(HALF + j * TILE, TILE), TILE)
        s1[:, cols] = merge(mm(choose, old_b[:, cols]), mm(choose, old_b[:, cols2]))
        return carry

    lax.fori_loop(0, HALF // TILE, choose_rows, 0)
    s1[:, HALF:] = merge(mm(choose, low_t, NT_DIMS), mm(choose, high_t, NT_DIMS))

    group_me = y * 4 + z
    across = [(i, j) for i in (2, 1, 3, 0) for j in (2, 1, 3, 0) if i or j]
    for i, j in across:
        g = lax.rem(y + i, 4) * 4 + lax.rem(z + j, 4)
        send(("yz", i, j), s1.at[span(g, 16)], b1.at[span(group_me, 16)], at(z + j, x, c, y + i))
    own_yz = local(s1.at[span(group_me, 16)], b1.at[span(group_me, 16)])

    def keep_rows(cols):
        high = old_b[:, cols]
        rest = old_f[:, cols] - high.astype(F32)
        mid = rest.astype(BF16)
        low = (rest - mid.astype(F32)).astype(BF16)
        old_f[:, cols] = (mm(keep_t, high) + mm(keep_t, mid)) + mm(keep_t, low)

    def clear(j, carry):
        acc[span(j, 64), :] = jnp.zeros((64, 512), F32)
        return carry

    lax.fori_loop(0, TOK // 64, clear, 0)

    lax.fori_loop(0, 6, lambda j, t: (keep_rows(span(j, TILE)), t)[1], 0)

    for colour, step in both:
        ag_recv(colour, "f", step, 0, 0)
        ag_send(colour, "f", step, -step, 0, part(step))
        for step2 in (1, -1):
            ag_send(colour, "s", step2, -step, 0)
    for colour, step in both:
        ag_recv(colour, "s", step, 0, 0)
        ag_send(colour, "s", step, 0, -step, part(step))

    lax.fori_loop(6, D // TILE, lambda j, t: (keep_rows(span(j, TILE)), t)[1], 0)

    own_yz.wait()
    for i, j in across:
        g = lax.rem(y + 4 - i, 4) * 4 + lax.rem(z + 4 - j, 4)
        receive(("yz", i, j), b1.at[span(g, 16)])

    r2 = iota((DEVICES, 256), 0)
    from_row = (r2 & 15) * 16 + (r2 >> 4)
    perm_l = one_hot(iota((DEVICES, 256), 1) == from_row)
    perm_r = one_hot(iota((DEVICES, 256), 1) == from_row + 8)

    def regroup(j, carry):
        cols = span(j, TILE)
        cols2 = pl.ds(pl.multiple_of(HALF + j * TILE, TILE), TILE)
        piece = b1[:, cols]
        s2[:, cols] = mm(perm_l, piece).astype(BF16)
        s2[:, cols2] = mm(perm_r, piece).astype(BF16)
        return carry

    lax.fori_loop(0, HALF // TILE, regroup, 0)
    s2[:, D : D + 128] = mm(perm_l, b1[:, HALF:]).astype(BF16)
    s2[:, D + 128 :] = mm(perm_r, b1[:, HALF:]).astype(BF16)

    e_me = x * 2 + c
    for m in (4, 3, 5, 2, 6, 1, 7):
        e = lax.rem(e_me + m, 8)
        send(("xc", m), s2.at[span(e, 16)], b3.at[span(e_me, 16)], at(z, lax.div(e, 2), lax.rem(e, 2)))
    own_xc = local(s2.at[span(e_me, 16)], b3.at[span(e_me, 16)])

    send("hid", hid_ref, hid_y, at(z, x, c, y + 1))
    send("gains", gains_ref, gains_y, at(z, x, c, y + 1))

    for colour in (0, 1):
        for step in (1, -1):
            ag_recv(colour, "f", step, -step, 0, part(step))
        for step in (1, -1):
            ag_send(colour, "s", step, 2, 0)
    for fk in (-1, 1):
        for colour, step in both:
            ag_recv(colour, "s", step, fk, 0)
            ag_send(colour, "s", step, fk, -step, part(step))

    own_xc.wait()
    for m in (4, 3, 5, 2, 6, 1, 7):
        receive(("xc", m), b3.at[span(lax.rem(e_me + 8 - m, 8), 16)])

    low_lab = b3[:, D : D + 128]
    high_lab = b3[:, D + 128 :]
    arrived = jnp.concatenate([low_lab * high_lab[:, a : a + 1] for a in range(3)], axis=1)

    def place_rows(cols):
        m = old_f[:, cols] + mm(arrived, b3[:, cols], TN_DIMS)
        old_f[:, cols] = m
        w[:, cols] = m.astype(BF16)

    tiles(D // TILE, place_rows)
    master_copy = local(old_f, master_hbm)

    theirs = span(1 - c, HALF)
    ours = span(c, HALF)
    k_rows = pl.ds(pl.multiple_of(256 + 64 * c, 64), 64)
    v_rows = pl.ds(pl.multiple_of(384 + 64 * c, 64), 64)
    k_rows_p = pl.ds(pl.multiple_of(256 + 64 * (1 - c), 64), 64)
    v_rows_p = pl.ds(pl.multiple_of(384 + 64 * (1 - c), 64), 64)
    o_rows = span(c, 128)
    o_rows_p = span(1 - c, 128)
    send("wq", w.at[0:128, theirs], wp.at[128:256], partner)
    send("wk", w.at[128:192, theirs], wp.at[k_rows], partner)
    send("wv", w.at[192:256, theirs], wp.at[v_rows], partner)
    send("wo", w.at[256:384], of.at[o_rows], partner)
    own_w = [
        local(w.at[0:128, ours], wp.at[0:128]),
        local(w.at[128:192, ours], wp.at[k_rows]),
        local(w.at[192:256, ours], wp.at[v_rows]),
        local(w.at[256:384], of.at[o_rows]),
    ]

    for colour, step in both:
        ag_recv(colour, "s", step, 2, 0)
        ag_send(colour, "s", step, 2, -step, part(step))

    for copy in own_w:
        copy.wait()
    receive("wq", wp.at[128:256])
    receive("wk", wp.at[k_rows_p])
    receive("wv", wp.at[v_rows_p])
    receive("wo", of.at[o_rows_p])

    fi = x + c * (z - x)
    si = z + c * (x - z)

    def along_f(k, yy=y):
        return at(z + c * k, x + (1 - c) * k, c, yy)

    def along_s(k):
        return at(z + (1 - c) * k, x + c * k, c)

    for k in (2, 1, 3):
        send(("ow", k), of.at[:, span(lax.rem(fi + k, 4), QUARTER)], ow.at[fi], along_f(k))
    own_o = local(of.at[:, span(fi, QUARTER)], ow.at[fi])

    def project(colour, fk):
        if colour == 0:
            xx = lax.rem(x + fk + 4, 4)
            places = [pl.ds(pl.multiple_of((q * 4 + xx) * 128, 128), 128) for q in range(4)]
        else:
            zz = lax.rem(z + fk + 4, 4)
            places = [pl.ds(pl.multiple_of((zz * 4 + q) * 128, 128), 128) for q in range(4)]
        cols = slice(colour * COLOR, (colour + 1) * COLOR)
        block = jnp.concatenate([xg[p, cols] for p in places], axis=0)
        out = mm(block, wp[:, cols], NT_DIMS)
        for q, p in enumerate(places):
            piece = out[q * 128 : (q + 1) * 128]
            acc[p, :] = acc[p, :] + piece

    for fk in (0, -1, 1, 2):
        for colour in (0, 1):
            for step in (1, -1):
                ag_recv(colour, "s", step, fk, -step, part(step))
            project(colour, fk)

    for g in range(4):
        at_rows = pl.ds(g * GROUP, GROUP)
        psend[at_rows, :] = acc[at_rows, 128:512].astype(BF16)
        send(("proj", g), psend.at[at_rows], precv.at[at_rows], partner)

    def combine(g):
        at_rows = pl.ds(g * GROUP, GROUP)
        receive(("proj", g), precv.at[at_rows])
        q = acc[at_rows, 0:128] + precv[at_rows, 0:128].astype(F32)
        kv = acc[at_rows, 256:512] + precv[at_rows, 128:384].astype(F32)
        z_qkv[at_rows, 0:128] = (q * score_scale).astype(BF16)
        z_qkv[at_rows, 128:384] = kv.astype(BF16)

    def attend(qb):
        q = z_qkv[qb * QB : (qb + 1) * QB, 0:128]
        peak = None
        for kb in range(qb + 1):
            cols = slice(kb * QB, (kb + 1) * QB)
            s = mm(q, z_qkv[cols, 128:256], NT_DIMS)
            if kb == qb:
                s = jnp.where(iota((QB, QB), 0) >= iota((QB, QB), 1), s, -1e30)
            sc[:, cols] = s
            top = jnp.maximum(s[:, 0:128], s[:, 128:256])
            peak = top if peak is None else jnp.maximum(peak, top)
        peak = jnp.max(peak, axis=-1, keepdims=True)
        total = None
        out = None
        for kb in range(qb + 1):
            cols = slice(kb * QB, (kb + 1) * QB)
            e = jnp.exp2(sc[:, cols] - peak)
            add = e[:, 0:128] + e[:, 128:256]
            total = add if total is None else total + add
            o = mm(e.astype(BF16), z_qkv[cols, 256:384])
            out = o if out is None else out + o
        total = jnp.sum(total, axis=-1, keepdims=True)
        out = (out / total).astype(BF16)
        for i in range(QB // 128):
            ci = qb * (QB // 128) + i
            for core in range(2):
                for half in range(2):
                    first = i * 128 + core * 64 + half * 32
                    at_row = half * 512 + ci * 32
                    att[core, at_row : at_row + 32, :] = out[first : first + 32]

    head_cols = span(c, 128)
    head_cols_p = span(1 - c, 128)
    own_a = {}

    def f_at(k):
        return lax.rem(fi + k + 4, 4)

    def rows_g(g, half=None):
        return pl.ds(g * 512, 512) if half is None else pl.ds(g * 512 + half * 256, 256)

    def gather_1(g):
        send(("att", g), att.at[1 - c, rows_g(g)], hg.at[si, rows_g(g), head_cols], partner)
        own_a[g] = local(att.at[c, rows_g(g)], hg.at[fi, rows_g(g), head_cols])

    def gather_2(g):
        own_a[g].wait()
        receive(("att", g), hg.at[fi, rows_g(g), head_cols_p])
        for step in (1, -1):
            ref = hg.at[fi, rows_g(g)]
            send(("hg", step, g), ref, ref, along_f(step))

    def gather_3(g):
        for step in (1, -1):
            receive(("hg", step, g), hg.at[f_at(-step), rows_g(g)])
            ref = hg.at[f_at(-step), rows_g(g, part(step))]
            send(("hg2", step, g), ref, ref, along_f(step))

    for g in range(4):
        combine(g)
        attend(2 * g)
        attend(2 * g + 1)

    def products(g):
        for step in (1, -1):
            receive(("hg2", step, g), hg.at[f_at(2), rows_g(g, part(step))])

        def columns(cols):
            out = None
            for f in range(4):
                o = mm(hg[f, rows_g(g), :], ow[f, :, cols])
                out = o if out is None else out + o
            part_f[rows_g(g), cols] = out

        tiles(QUARTER // TILE, columns)

    def source(j, q, g):
        s_there = lax.rem(si + j + 4, 4)
        block = s_there * (4 - 3 * c) + q * (1 + 3 * c)
        return pl.ds(pl.multiple_of(g * 512 + block * 32, 32), 32)

    def half_rows(g):
        return pl.ds(g * 64, 64)

    def all_rows(g):
        return pl.ds(g * 128, 128)

    def q_rows(g, q):
        return pl.ds(g * 128 + q * 32, 32)

    def reduce_1(g):
        for q in range(4):
            ps[0, q_rows(g, q), :] = part_f[source(2, q, g), :].astype(BF16)
        for step in (1, -1):
            src = ps.at[0, pl.ds(g * 128 + part(step) * 64, 64)]
            send(("rh", step, g), src, rh.at[part(step), half_rows(g)], along_s(step))

    def reduce_2(g):
        for step in (1, -1):
            h_in = part(step)
            n = 1 + h_in
            for q in range(4):
                if q // 2 != h_in:
                    ps[n, q_rows(g, q), :] = part_f[source(step, q, g), :].astype(BF16)
            receive(("rh", step, g), rh.at[h_in, half_rows(g)])
            for q in range(4):
                if q // 2 == h_in:
                    came = rh[h_in, pl.ds(g * 64 + (q % 2) * 32, 32), :].astype(F32)
                    ps[n, q_rows(g, q), :] = (part_f[source(step, q, g), :] + came).astype(BF16)
            send(("rf", step, g), ps.at[n, all_rows(g)], rf.at[h_in, all_rows(g)], along_s(step))

    order = (2, 1, 3, 0)

    def reduce_3(g):
        for step in (1, -1):
            receive(("rf", step, g), rf.at[part(step), all_rows(g)])
        for q in range(4):
            rows_q = q_rows(g, q)
            came = rf[0, rows_q, :].astype(F32) + rf[1, rows_q, :].astype(F32)
            mx[rows_q, :] = (part_f[source(0, q, g), :] + came).astype(BF16)
        for k in order:
            src = mx.at[pl.ds(pl.multiple_of(g * 128 + f_at(k) * 32, 32), 32)]
            send(("mx", k, g), src, mixed.at[pl.ds(g * 32, 32), span(fi, QUARTER)], along_f(k, y + 1))

    def finish(g):
        at_rows = pl.ds(g * 32, 32)
        for k in order:
            receive(("mx", k, g), mixed.at[at_rows, span(lax.rem(fi + 4 - k, 4), QUARTER)])
        m = mixed[at_rows, :].astype(F32)
        scale2 = lax.rsqrt(jnp.mean(m * m, axis=-1, keepdims=True) + epsilon)
        out_ref[at_rows, :] = (hid_y[at_rows, :].astype(F32) + m * scale2 * gains_y[1:2, :]).astype(BF16)

    gather_1(0)
    gather_1(1)
    gather_2(0)
    gather_3(0)
    gather_2(1)
    own_o.wait()
    for k in (1, 3, 2):
        receive(("ow", k), ow.at[lax.rem(fi + 4 - k, 4)])
    products(0)
    reduce_1(0)
    gather_3(1)
    reduce_2(0)
    products(1)
    reduce_1(1)
    reduce_3(0)
    reduce_2(1)
    reduce_3(1)
    receive("hid", hid_y)
    receive("gains", gains_y)
    finish(0)
    finish(1)

    master_copy.wait()
    for copy in sent:
        copy.wait_send()


def layer(old_master, rows, gains, hidden):
    vmem = pl.BlockSpec(memory_space=pltpu.VMEM)
    anywhere = pl.BlockSpec(memory_space=pl.ANY)
    return pl.pallas_call(
        layer_kernel,
        out_shape=(
            jax.ShapeDtypeStruct((SLAB, D), F32),
            jax.ShapeDtypeStruct((OWN_TOK, D), BF16),
        ),
        in_specs=[anywhere, vmem, vmem, vmem],
        out_specs=(anywhere, vmem),
        scratch_shapes=[
            pltpu.VMEM((SLAB, D), F32),
            pltpu.VMEM((SLAB, D), BF16),
            pltpu.VMEM((256, PIECE), BF16),
            pltpu.VMEM((256, PIECE), BF16),
            pltpu.VMEM((DEVICES, 2 * PIECE), BF16),
            pltpu.VMEM((DEVICES, 2 * PIECE), BF16),
            pltpu.VMEM((SLAB, D), BF16),
            pltpu.VMEM((512, HALF), BF16),
            pltpu.VMEM((OWN_TOK, D), BF16),
            pltpu.VMEM((TOK, HALF), BF16),
            pltpu.VMEM((TOK, 512), F32),
            pltpu.VMEM((TOK, 384), BF16),
            pltpu.VMEM((TOK, 384), BF16),
            pltpu.VMEM((TOK, 384), BF16),
            pltpu.VMEM((2, TOK // 2, 128), BF16),
            pltpu.VMEM((4, TOK // 2, 256), BF16),
            pltpu.VMEM((256, D), BF16),
            pltpu.VMEM((4, 256, QUARTER), BF16),
            pltpu.VMEM((QB, TOK), F32),
            pltpu.VMEM((TOK // 2, QUARTER), F32),
            pltpu.VMEM((3, 256, QUARTER), BF16),
            pltpu.VMEM((2, 128, QUARTER), BF16),
            pltpu.VMEM((2, 256, QUARTER), BF16),
            pltpu.VMEM((256, QUARTER), BF16),
            pltpu.VMEM((OWN_TOK, D), BF16),
            pltpu.VMEM((OWN_TOK, D), BF16),
            pltpu.VMEM((2, D), F32),
            pltpu.SemaphoreType.DMA((3,)),
            pltpu.SemaphoreType.DMA((16,)),
            pltpu.SemaphoreType.DMA((128,)),
            pltpu.SemaphoreType.DMA((128,)),
        ],
        compiler_params=pltpu.CompilerParams(
            collective_id=0, has_side_effects=True, vmem_limit_bytes=63 * 1024 * 1024
        ),
    )(old_master, rows, gains, hidden)


def body(old_master, old_rows, gains, hidden_in):
    master, hidden_out = layer(old_master, old_rows, gains[0], hidden_in[0])
    return (master, hidden_out[None])


def solution(mesh):
    in_specs = (
        P(("section", "dp"), None),
        P(("section", "dp")),
        P("section", None, None),
        P("section", "dp", None),
    )
    out_specs = (P(("section", "dp"), None), P("section", "dp", None))
    return jax.shard_map(body, mesh=mesh, in_specs=in_specs, out_specs=out_specs, check_vma=False)
```

```python
import jax
import jax.numpy as jnp
from jax import lax
from jax.experimental import pallas as pl
from jax.experimental.pallas import tpu as pltpu
from jax.sharding import PartitionSpec as P

MESH = pl.DeviceIdType.MESH
F32 = jnp.float32
BF16 = jnp.bfloat16

D = 4608
HD = 128
SLAB = 384
TOK = 2048
OWN_TOK = 64
HALF = D // 2
COLOR = HALF // 2
QUARTER = D // 4
DEVICES = 128
PIECE = HALF + 128
TILE = 384
GROUP = 512
QB = 256

epsilon = 1e-06
LOG2E = 1.4426950408889634
score_scale = LOG2E / 12.0

NT_DIMS = (((1,), (1,)), ((), ()))
TN_DIMS = (((0,), (0,)), ((), ()))


def iota(shape, dim):
    return lax.broadcasted_iota(jnp.int32, shape, dim)


def one_hot(mask):
    return jnp.where(mask, 1.0, 0.0).astype(BF16)


def mm(a, b, dims=None):
    if dims is None:
        return jnp.dot(a, b, preferred_element_type=F32)
    return lax.dot_general(a, b, dims, preferred_element_type=F32)


def span(index, size):
    return pl.ds(pl.multiple_of(index * size, size), size)


def merge(left, right):
    n = left.shape[1]
    pair = jnp.concatenate([left.reshape(16, 8, n), right.reshape(16, 8, n)], axis=1)
    return pair.reshape(256, n).astype(BF16)


def layer_kernel(
    old_hbm, rows_ref, gains_ref, hid_ref, master_hbm, out_ref,
    old_f, old_b, s1, b1, s2, b3, w, wp, nrm, xg, acc, psend, precv, z_qkv,
    att, hg, of, ow, sc, part_f, ps, rh, rf, mx, mixed, hid_y, gains_y,
    load_sem, loc_sem, send_sem, recv_sem,
):
    y = lax.axis_index("section")
    d = lax.axis_index("dp")
    c = lax.rem(d, 2)
    chip = lax.div(d, 2)
    x = lax.rem(chip, 4)
    z = lax.div(chip, 4)
    me = y * 32 + d

    def at(zz, xx, cc, yy=y):
        return (lax.rem(yy + 4, 4), (lax.rem(zz + 4, 4) * 4 + lax.rem(xx + 4, 4)) * 2 + cc)

    partner = at(z, x, 1 - c)
    ids = {}
    sent = []

    def slot(key):
        return ids.setdefault(key, len(ids))

    def send(key, src, dst, dev):
        n = slot(key)
        copy = pltpu.make_async_remote_copy(
            src_ref=src, dst_ref=dst, send_sem=send_sem.at[n], recv_sem=recv_sem.at[n],
            device_id=dev, device_id_type=MESH,
        )
        copy.start()
        sent.append(copy)

    def receive(key, dst):
        n = slot(key)
        pltpu.make_async_remote_copy(
            src_ref=dst, dst_ref=dst, send_sem=send_sem.at[n], recv_sem=recv_sem.at[n],
            device_id=partner, device_id_type=MESH,
        ).wait_recv()

    local_count = [0]

    def local(src, dst):
        copy = pltpu.make_async_copy(src, dst, loc_sem.at[local_count[0]])
        local_count[0] += 1
        copy.start()
        return copy

    def load(i):
        at_rows = pl.ds(i * 128, 128)
        return pltpu.make_async_copy(old_hbm.at[at_rows], old_f.at[at_rows], load_sem.at[i])

    for i in range(3):
        load(i).start()

    barrier = pltpu.get_barrier_semaphore()
    greeted = [at(z + j, x, c, y + i) for i in range(4) for j in range(4) if i or j]
    greeted += [at(z, x, 1 - c)]
    for k in (1, 2, 3):
        greeted += [at(z, x + k, c), at(z, x + k, 1 - c), at(z, x + k, c, y + 1), at(z, x + k, c, y + 3)]
    for dev in greeted:
        pl.semaphore_signal(barrier, inc=1, device_id=dev, device_id_type=MESH)

    h = hid_ref[...].astype(F32)
    scale = lax.rsqrt(jnp.mean(h * h, axis=-1, keepdims=True) + epsilon)
    nrm[...] = (h * scale * gains_ref[0:1, :]).astype(BF16)
    pl.semaphore_wait(barrier, len(greeted))

    own_rows = pl.ds(pl.multiple_of(chip * 128 + c * 64, 64), 64)
    other_rows = pl.ds(pl.multiple_of(chip * 128 + (1 - c) * 64, 64), 64)
    send("norm", nrm.at[:, span(1 - c, HALF)], xg.at[own_rows], partner)
    own_copy = local(nrm.at[:, span(c, HALF)], xg.at[own_rows])

    def ag_place(colour, fk, sk, half):
        if colour == 0:
            cc = lax.rem(z + sk + 4, 4) * 4 + lax.rem(x + fk + 4, 4)
        else:
            cc = lax.rem(z + fk + 4, 4) * 4 + lax.rem(x + sk + 4, 4)
        if half is None:
            rows = pl.ds(pl.multiple_of(cc * 128, 128), 128)
        else:
            rows = pl.ds(pl.multiple_of(cc * 128 + half * 64, 64), 64)
        return xg.at[rows, pl.ds(colour * COLOR, COLOR)]

    def ag_send(colour, axis, step, fk, sk, half=None):
        along_x = (axis == "f") == (colour == 0)
        dev = at(z, x + step, c) if along_x else at(z + step, x, c)
        ref = ag_place(colour, fk, sk, half)
        send(("ag", colour, axis, step, fk % 4, sk % 4, half), ref, ref, dev)

    def ag_recv(colour, axis, step, fk, sk, half=None):
        key = ("ag", colour, axis, step, fk % 4, sk % 4, half)
        if axis == "f":
            fk = (fk - step) % 4
        else:
            sk = (sk - step) % 4
        receive(key, ag_place(colour, fk, sk, half))

    def part(step):
        return 0 if step == 1 else 1

    both = [(colour, step) for colour in (0, 1) for step in (1, -1)]

    def tiles(count, body, size=TILE):
        def one(j, carry):
            body(span(j, size))
            return carry

        lax.fori_loop(0, count, one, 0)

    own_copy.wait()
    receive("norm", xg.at[other_rows])
    for colour, step in both:
        ag_send(colour, "f", step, 0, 0)
    for colour, step in both:
        ag_send(colour, "s", step, 0, 0)

    rows = rows_ref[...].reshape(1, SLAB)
    owner = jnp.floor((rows.astype(F32) + 0.5) * (1.0 / SLAB)).astype(jnp.int32)
    place = rows - owner * SLAB
    dest = iota((DEVICES, SLAB), 0)
    choose = one_hot((owner == dest) & (dest != me))
    keep_t = one_hot((rows - me * SLAB) == iota((SLAB, SLAB), 0))
    low_t = one_hot((place & 127) == iota((128, SLAB), 0))
    high_t = one_hot((place >> 7) == iota((128, SLAB), 0))
    for i in range(3):
        load(i).wait()

        def cast(j, carry):
            at_rows = pl.ds(pl.multiple_of(i * 128 + j * 16, 16), 16)
            old_b[at_rows, :] = old_f[at_rows, :].astype(BF16)
            return carry

        lax.fori_loop(0, 8, cast, 0)

    def choose_rows(j, carry):
        cols = span(j, TILE)
        cols2 = pl.ds(pl.multiple_of(HALF + j * TILE, TILE), TILE)
        s1[:, cols] = merge(mm(choose, old_b[:, cols]), mm(choose, old_b[:, cols2]))
        return carry

    lax.fori_loop(0, HALF // TILE, choose_rows, 0)
    s1[:, HALF:] = merge(mm(choose, low_t, NT_DIMS), mm(choose, high_t, NT_DIMS))

    group_me = y * 4 + z
    across = [(i, j) for i in (2, 1, 3, 0) for j in (2, 1, 3, 0) if i or j]
    for i, j in across:
        g = lax.rem(y + i, 4) * 4 + lax.rem(z + j, 4)
        send(("yz", i, j), s1.at[span(g, 16)], b1.at[span(group_me, 16)], at(z + j, x, c, y + i))
    own_yz = local(s1.at[span(group_me, 16)], b1.at[span(group_me, 16)])

    def keep_rows(cols):
        high = old_b[:, cols]
        rest = old_f[:, cols] - high.astype(F32)
        mid = rest.astype(BF16)
        low = (rest - mid.astype(F32)).astype(BF16)
        old_f[:, cols] = (mm(keep_t, high) + mm(keep_t, mid)) + mm(keep_t, low)

    def clear(j, carry):
        acc[span(j, 64), :] = jnp.zeros((64, 512), F32)
        return carry

    lax.fori_loop(0, TOK // 64, clear, 0)

    lax.fori_loop(0, 6, lambda j, t: (keep_rows(span(j, TILE)), t)[1], 0)

    for colour, step in both:
        ag_recv(colour, "f", step, 0, 0)
        ag_send(colour, "f", step, -step, 0, part(step))
        for step2 in (1, -1):
            ag_send(colour, "s", step2, -step, 0)
    for colour, step in both:
        ag_recv(colour, "s", step, 0, 0)
        ag_send(colour, "s", step, 0, -step, part(step))

    lax.fori_loop(6, D // TILE, lambda j, t: (keep_rows(span(j, TILE)), t)[1], 0)

    own_yz.wait()
    for i, j in across:
        g = lax.rem(y + 4 - i, 4) * 4 + lax.rem(z + 4 - j, 4)
        receive(("yz", i, j), b1.at[span(g, 16)])

    r2 = iota((DEVICES, 256), 0)
    from_row = (r2 & 15) * 16 + (r2 >> 4)
    perm_l = one_hot(iota((DEVICES, 256), 1) == from_row)
    perm_r = one_hot(iota((DEVICES, 256), 1) == from_row + 8)

    def regroup(j, carry):
        cols = span(j, TILE)
        cols2 = pl.ds(pl.multiple_of(HALF + j * TILE, TILE), TILE)
        piece = b1[:, cols]
        s2[:, cols] = mm(perm_l, piece).astype(BF16)
        s2[:, cols2] = mm(perm_r, piece).astype(BF16)
        return carry

    lax.fori_loop(0, HALF // TILE, regroup, 0)
    s2[:, D : D + 128] = mm(perm_l, b1[:, HALF:]).astype(BF16)
    s2[:, D + 128 :] = mm(perm_r, b1[:, HALF:]).astype(BF16)

    e_me = x * 2 + c
    for m in (4, 3, 5, 2, 6, 1, 7):
        e = lax.rem(e_me + m, 8)
        send(("xc", m), s2.at[span(e, 16)], b3.at[span(e_me, 16)], at(z, lax.div(e, 2), lax.rem(e, 2)))
    own_xc = local(s2.at[span(e_me, 16)], b3.at[span(e_me, 16)])

    send("hid", hid_ref, hid_y, at(z, x, c, y + 1))
    send("gains", gains_ref, gains_y, at(z, x, c, y + 1))

    for colour in (0, 1):
        for step in (1, -1):
            ag_recv(colour, "f", step, -step, 0, part(step))
        for step in (1, -1):
            ag_send(colour, "s", step, 2, 0)
    for fk in (-1, 1):
        for colour, step in both:
            ag_recv(colour, "s", step, fk, 0)
            ag_send(colour, "s", step, fk, -step, part(step))

    own_xc.wait()
    for m in (4, 3, 5, 2, 6, 1, 7):
        receive(("xc", m), b3.at[span(lax.rem(e_me + 8 - m, 8), 16)])

    low_lab = b3[:, D : D + 128]
    high_lab = b3[:, D + 128 :]
    arrived = jnp.concatenate([low_lab * high_lab[:, a : a + 1] for a in range(3)], axis=1)

    def place_rows(cols):
        m = old_f[:, cols] + mm(arrived, b3[:, cols], TN_DIMS)
        old_f[:, cols] = m
        w[:, cols] = m.astype(BF16)

    tiles(D // TILE, place_rows)
    master_copy = local(old_f, master_hbm)

    theirs = span(1 - c, HALF)
    ours = span(c, HALF)
    k_rows = pl.ds(pl.multiple_of(256 + 64 * c, 64), 64)
    v_rows = pl.ds(pl.multiple_of(384 + 64 * c, 64), 64)
    k_rows_p = pl.ds(pl.multiple_of(256 + 64 * (1 - c), 64), 64)
    v_rows_p = pl.ds(pl.multiple_of(384 + 64 * (1 - c), 64), 64)
    o_rows = span(c, 128)
    o_rows_p = span(1 - c, 128)
    send("wq", w.at[0:128, theirs], wp.at[128:256], partner)
    send("wk", w.at[128:192, theirs], wp.at[k_rows], partner)
    send("wv", w.at[192:256, theirs], wp.at[v_rows], partner)
    send("wo", w.at[256:384], of.at[o_rows], partner)
    own_w = [
        local(w.at[0:128, ours], wp.at[0:128]),
        local(w.at[128:192, ours], wp.at[k_rows]),
        local(w.at[192:256, ours], wp.at[v_rows]),
        local(w.at[256:384], of.at[o_rows]),
    ]

    for colour, step in both:
        ag_recv(colour, "s", step, 2, 0)
        ag_send(colour, "s", step, 2, -step, part(step))

    for copy in own_w:
        copy.wait()
    receive("wq", wp.at[128:256])
    receive("wk", wp.at[k_rows_p])
    receive("wv", wp.at[v_rows_p])
    receive("wo", of.at[o_rows_p])

    fi = x + c * (z - x)
    si = z + c * (x - z)

    def along_f(k, yy=y):
        return at(z + c * k, x + (1 - c) * k, c, yy)

    def along_s(k):
        return at(z + (1 - c) * k, x + c * k, c)

    for k in (2, 1, 3):
        send(("ow", k), of.at[:, span(lax.rem(fi + k, 4), QUARTER)], ow.at[fi], along_f(k))
    own_o = local(of.at[:, span(fi, QUARTER)], ow.at[fi])

    def project(colour, fk):
        if colour == 0:
            xx = lax.rem(x + fk + 4, 4)
            places = [pl.ds(pl.multiple_of((q * 4 + xx) * 128, 128), 128) for q in range(4)]
        else:
            zz = lax.rem(z + fk + 4, 4)
            places = [pl.ds(pl.multiple_of((zz * 4 + q) * 128, 128), 128) for q in range(4)]
        cols = slice(colour * COLOR, (colour + 1) * COLOR)
        block = jnp.concatenate([xg[p, cols] for p in places], axis=0)
        out = mm(block, wp[:, cols], NT_DIMS)
        for q, p in enumerate(places):
            piece = out[q * 128 : (q + 1) * 128]
            acc[p, :] = acc[p, :] + piece

    for fk in (0, -1, 1, 2):
        for colour in (0, 1):
            for step in (1, -1):
                ag_recv(colour, "s", step, fk, -step, part(step))
            project(colour, fk)

    for g in range(4):
        at_rows = pl.ds(g * GROUP, GROUP)
        psend[at_rows, :] = acc[at_rows, 128:512].astype(BF16)
        send(("proj", g), psend.at[at_rows], precv.at[at_rows], partner)

    def combine(g):
        at_rows = pl.ds(g * GROUP, GROUP)
        receive(("proj", g), precv.at[at_rows])
        q = acc[at_rows, 0:128] + precv[at_rows, 0:128].astype(F32)
        kv = acc[at_rows, 256:512] + precv[at_rows, 128:384].astype(F32)
        z_qkv[at_rows, 0:128] = (q * score_scale).astype(BF16)
        z_qkv[at_rows, 128:384] = kv.astype(BF16)

    def attend(qb):
        q = z_qkv[qb * QB : (qb + 1) * QB, 0:128]
        peak = None
        for kb in range(qb + 1):
            cols = slice(kb * QB, (kb + 1) * QB)
            s = mm(q, z_qkv[cols, 128:256], NT_DIMS)
            if kb == qb:
                s = jnp.where(iota((QB, QB), 0) >= iota((QB, QB), 1), s, -1e30)
            sc[:, cols] = s
            top = jnp.maximum(s[:, 0:128], s[:, 128:256])
            peak = top if peak is None else jnp.maximum(peak, top)
        peak = jnp.max(peak, axis=-1, keepdims=True)
        total = None
        out = None
        for kb in range(qb + 1):
            cols = slice(kb * QB, (kb + 1) * QB)
            e = jnp.exp2(sc[:, cols] - peak)
            add = e[:, 0:128] + e[:, 128:256]
            total = add if total is None else total + add
            o = mm(e.astype(BF16), z_qkv[cols, 256:384])
            out = o if out is None else out + o
        total = jnp.sum(total, axis=-1, keepdims=True)
        out = (out / total).astype(BF16)
        for i in range(QB // 128):
            ci = qb * (QB // 128) + i
            for core in range(2):
                for half in range(2):
                    first = i * 128 + core * 64 + half * 32
                    at_row = half * 512 + ci * 32
                    att[core, at_row : at_row + 32, :] = out[first : first + 32]

    head_cols = span(c, 128)
    head_cols_p = span(1 - c, 128)
    own_a = {}

    def f_at(k):
        return lax.rem(fi + k + 4, 4)

    def rows_g(g, half=None):
        return pl.ds(g * 512, 512) if half is None else pl.ds(g * 512 + half * 256, 256)

    def gather_1(g):
        send(("att", g), att.at[1 - c, rows_g(g)], hg.at[si, rows_g(g), head_cols], partner)
        own_a[g] = local(att.at[c, rows_g(g)], hg.at[fi, rows_g(g), head_cols])

    def gather_2(g):
        own_a[g].wait()
        receive(("att", g), hg.at[fi, rows_g(g), head_cols_p])
        for step in (1, -1):
            ref = hg.at[fi, rows_g(g)]
            send(("hg", step, g), ref, ref, along_f(step))

    def gather_3(g):
        for step in (1, -1):
            receive(("hg", step, g), hg.at[f_at(-step), rows_g(g)])
            ref = hg.at[f_at(-step), rows_g(g, part(step))]
            send(("hg2", step, g), ref, ref, along_f(step))

    for g in range(4):
        combine(g)
        attend(2 * g)
        attend(2 * g + 1)

    def products(g):
        for step in (1, -1):
            receive(("hg2", step, g), hg.at[f_at(2), rows_g(g, part(step))])

        def columns(cols):
            out = None
            for f in range(4):
                o = mm(hg[f, rows_g(g), :], ow[f, :, cols])
                out = o if out is None else out + o
            part_f[rows_g(g), cols] = out

        tiles(QUARTER // TILE, columns)

    def source(j, q, g):
        s_there = lax.rem(si + j + 4, 4)
        block = s_there * (4 - 3 * c) + q * (1 + 3 * c)
        return pl.ds(pl.multiple_of(g * 512 + block * 32, 32), 32)

    def half_rows(g):
        return pl.ds(g * 64, 64)

    def all_rows(g):
        return pl.ds(g * 128, 128)

    def q_rows(g, q):
        return pl.ds(g * 128 + q * 32, 32)

    def reduce_1(g):
        for q in range(4):
            ps[0, q_rows(g, q), :] = part_f[source(2, q, g), :].astype(BF16)
        for step in (1, -1):
            src = ps.at[0, pl.ds(g * 128 + part(step) * 64, 64)]
            send(("rh", step, g), src, rh.at[part(step), half_rows(g)], along_s(step))

    def reduce_2(g):
        for step in (1, -1):
            h_in = part(step)
            n = 1 + h_in
            for q in range(4):
                if q // 2 != h_in:
                    ps[n, q_rows(g, q), :] = part_f[source(step, q, g), :].astype(BF16)
            receive(("rh", step, g), rh.at[h_in, half_rows(g)])
            for q in range(4):
                if q // 2 == h_in:
                    came = rh[h_in, pl.ds(g * 64 + (q % 2) * 32, 32), :].astype(F32)
                    ps[n, q_rows(g, q), :] = (part_f[source(step, q, g), :] + came).astype(BF16)
            send(("rf", step, g), ps.at[n, all_rows(g)], rf.at[h_in, all_rows(g)], along_s(step))

    order = (2, 1, 3, 0)

    def reduce_3(g):
        for step in (1, -1):
            receive(("rf", step, g), rf.at[part(step), all_rows(g)])
        for q in range(4):
            rows_q = q_rows(g, q)
            came = rf[0, rows_q, :].astype(F32) + rf[1, rows_q, :].astype(F32)
            mx[rows_q, :] = (part_f[source(0, q, g), :] + came).astype(BF16)
        for k in order:
            src = mx.at[pl.ds(pl.multiple_of(g * 128 + f_at(k) * 32, 32), 32)]
            send(("mx", k, g), src, mixed.at[pl.ds(g * 32, 32), span(fi, QUARTER)], along_f(k, y + 1))

    def finish(g):
        at_rows = pl.ds(g * 32, 32)
        for k in order:
            receive(("mx", k, g), mixed.at[at_rows, span(lax.rem(fi + 4 - k, 4), QUARTER)])
        m = mixed[at_rows, :].astype(F32)
        scale2 = lax.rsqrt(jnp.mean(m * m, axis=-1, keepdims=True) + epsilon)
        out_ref[at_rows, :] = (hid_y[at_rows, :].astype(F32) + m * scale2 * gains_y[1:2, :]).astype(BF16)

    gather_1(0)
    gather_1(1)
    gather_2(0)
    gather_2(1)
    gather_3(0)
    own_o.wait()
    for k in (1, 3, 2):
        receive(("ow", k), ow.at[lax.rem(fi + 4 - k, 4)])
    products(0)
    reduce_1(0)
    gather_3(1)
    reduce_2(0)
    products(1)
    reduce_1(1)
    reduce_3(0)
    reduce_2(1)
    reduce_3(1)
    receive("hid", hid_y)
    receive("gains", gains_y)
    finish(0)
    finish(1)

    master_copy.wait()
    for copy in sent:
        copy.wait_send()


def layer(old_master, rows, gains, hidden):
    vmem = pl.BlockSpec(memory_space=pltpu.VMEM)
    anywhere = pl.BlockSpec(memory_space=pl.ANY)
    return pl.pallas_call(
        layer_kernel,
        out_shape=(
            jax.ShapeDtypeStruct((SLAB, D), F32),
            jax.ShapeDtypeStruct((OWN_TOK, D), BF16),
        ),
        in_specs=[anywhere, vmem, vmem, vmem],
        out_specs=(anywhere, vmem),
        scratch_shapes=[
            pltpu.VMEM((SLAB, D), F32),
            pltpu.VMEM((SLAB, D), BF16),
            pltpu.VMEM((256, PIECE), BF16),
            pltpu.VMEM((256, PIECE), BF16),
            pltpu.VMEM((DEVICES, 2 * PIECE), BF16),
            pltpu.VMEM((DEVICES, 2 * PIECE), BF16),
            pltpu.VMEM((SLAB, D), BF16),
            pltpu.VMEM((512, HALF), BF16),
            pltpu.VMEM((OWN_TOK, D), BF16),
            pltpu.VMEM((TOK, HALF), BF16),
            pltpu.VMEM((TOK, 512), F32),
            pltpu.VMEM((TOK, 384), BF16),
            pltpu.VMEM((TOK, 384), BF16),
            pltpu.VMEM((TOK, 384), BF16),
            pltpu.VMEM((2, TOK // 2, 128), BF16),
            pltpu.VMEM((4, TOK // 2, 256), BF16),
            pltpu.VMEM((256, D), BF16),
            pltpu.VMEM((4, 256, QUARTER), BF16),
            pltpu.VMEM((QB, TOK), F32),
            pltpu.VMEM((TOK // 2, QUARTER), F32),
            pltpu.VMEM((3, 256, QUARTER), BF16),
            pltpu.VMEM((2, 128, QUARTER), BF16),
            pltpu.VMEM((2, 256, QUARTER), BF16),
            pltpu.VMEM((256, QUARTER), BF16),
            pltpu.VMEM((OWN_TOK, D), BF16),
            pltpu.VMEM((OWN_TOK, D), BF16),
            pltpu.VMEM((2, D), F32),
            pltpu.SemaphoreType.DMA((3,)),
            pltpu.SemaphoreType.DMA((16,)),
            pltpu.SemaphoreType.DMA((128,)),
            pltpu.SemaphoreType.DMA((128,)),
        ],
        compiler_params=pltpu.CompilerParams(
            collective_id=0, has_side_effects=True, vmem_limit_bytes=63 * 1024 * 1024
        ),
    )(old_master, rows, gains, hidden)


def body(old_master, old_rows, gains, hidden_in):
    master, hidden_out = layer(old_master, old_rows, gains[0], hidden_in[0])
    return (master, hidden_out[None])


def solution(mesh):
    in_specs = (
        P(("section", "dp"), None),
        P(("section", "dp")),
        P("section", None, None),
        P("section", "dp", None),
    )
    out_specs = (P(("section", "dp"), None), P("section", "dp", None))
    return jax.shard_map(body, mesh=mesh, in_specs=in_specs, out_specs=out_specs, check_vma=False)
```
